256 devices in a mesh: dom: 16 (over z, y_lo), grp: 16 (over y_hi, x, core).
Axes of the slice: x: 4, y: 4 (y_hi: 2, y_lo: 2; y = y_hi * 2 + y_lo), z: 8, core: 2. Of those that a mesh axis runs over, the one named last changes fastest.
Arguments:
- psi: float32 [1024, 32768], P('grp', 'dom'), may hold values from -0.078125 to 0.078125
- proj: float32 [16, 128, 2048], P('dom'), may hold values from -6 to 6
- offsets: int32 [16], P('dom'), may hold values from 0 to 112
- species: int32 [128], replicated, may hold values from 0 to 3
- augment_q: float32 [4, 8, 8], replicated, as said below
- rotation: float32 [1024, 1024], replicated, may hold values from -0.1875 to 0.1875
- occupation: float32 [1024], replicated, may hold values from 0.1 to 1
Outputs:
- new_psi: float32 [1024, 32768], P('grp', 'dom')
- density: float32 [32768], P(('dom', 'grp'))
- rho_ij: float32 [128, 64], replicated
The draws below stay inside these ranges and needn't reach their ends.
Inputs may be any that keep to these rules, and one draw needn't show every extreme that they name: augment_q[s] is symmetric with a positive diagonal that dominates each row.
All inputs are finite; a program needn't handle non-finite values.
Results may differ from the reference program's by a relative error of at most 0.0003.
Values sent between devices are 32-bit elements; how exact they have to be, the bound alone decides.
A program may use at most 128 MiB of HBM per device.

```python
import math
import jax
import jax.numpy as jnp
from jax import lax

NS = 1024
CELLS_DEV = 2048
NPA = 8
NSPEC = 4
WIN = 16
NA = 128
NCELLS = 32768
N_DOM = 16


def draw_augment_q(key, part):
    key = jax.random.fold_in(key, 7)
    first, second = jax.random.split(key)
    raw = jax.random.uniform(first, (NSPEC, NPA, NPA), jnp.float32, -0.1, 0.1)
    sym = 0.5 * (raw + jnp.transpose(raw, (0, 2, 1)))
    diag = jax.random.uniform(second, (NSPEC, NPA), jnp.float32, 1.0, 2.0)
    eye = jnp.eye(NPA, dtype=jnp.float32)[None, :, :]
    matrix = sym * (1.0 - eye) + diag[:, :, None] * eye
    return matrix * (16.0 / (NA * NPA))


def touch_ends(entries, key, low, top_value):
    longest = entries.shape.index(max(entries.shape))
    spots = []
    for shift in (0, 1):
        where = [jax.random.randint(jax.random.fold_in(key, axis), (), 0, length) for axis, length in enumerate(entries.shape)]
        where[longest] = (where[longest] + shift) % entries.shape[longest]
        spots.append(tuple(where))
    return entries.at[spots[0]].set(low).at[spots[1]].set(top_value)


def steps_of(rng, dims, shards, smallest, largest):
    def one(dim, shards_of):
        draws = jax.random.uniform(jax.random.fold_in(jax.random.fold_in(rng, 6), dim), (shards_of,), jnp.float32, smallest / len(shards), largest / len(shards))
        return jnp.repeat(jnp.exp(draws), dims[dim] // shards_of).reshape((-1,) + (1,) * (len(dims) - dim - 1))

    gain = one(*shards[0])
    for cut in shards[1:]:
        gain = gain * one(*cut)
    return gain


def normal_values(key, shape, spread, most, cuts=(), kind=jnp.bfloat16):
    loudness = steps_of(key, shape, cuts, -0.22, 0.18) if cuts else 1.0
    entries = jax.random.normal(key, shape, jnp.float32) * spread * loudness
    return jnp.minimum(jnp.maximum(entries, -most), most).astype(kind)


def setup_inputs(seed: int = 0) -> dict:
    splits = jax.random.split(jax.random.key(seed), 8)
    return {
        "psi": normal_values(splits[0], (NS, NCELLS), (NCELLS ** -0.5), 0.078125, ((0, 16), (1, 16)), jnp.float32),
        "proj": normal_values(splits[1], (N_DOM, WIN * NPA, CELLS_DEV), 1.0, 6.0, ((0, 16),), jnp.float32),
        "offsets": touch_ends(jax.random.randint(splits[2], (N_DOM,), 0, NA - WIN + 1), jax.random.fold_in(splits[2], 1), 0, NA - WIN).astype(jnp.int32),
        "species": touch_ends(jax.random.randint(splits[3], (NA,), 0, NSPEC), jax.random.fold_in(splits[3], 1), 0, NSPEC - 1).astype(jnp.int32),
        "augment_q": draw_augment_q(jax.random.fold_in(splits[7], 71), 0),
        "rotation": normal_values(splits[5], (NS, NS), NS ** -0.5, 0.1875, (), jnp.float32),
        "occupation": jnp.clip(jnp.exp(jax.random.uniform(splits[6], (NS,), jnp.float32, math.log(0.1), math.log(1.0))), 0.1, 1.0),
    }


highest = lax.Precision.HIGHEST

def product(left, right):
    return jnp.dot(left.astype(jnp.float32), right.astype(jnp.float32), precision=highest, preferred_element_type=jnp.float32)

def reference(psi, proj, offsets, species, augment_q, rotation, occupation):
    columns = NA * NPA
    blocks = jnp.transpose(psi.reshape(NS, N_DOM, CELLS_DEV), (1, 0, 2))

    def add_domain(coeff, inputs):
        block, values, start = inputs
        partial_value = product(block, values.T)
        placed = lax.dynamic_update_slice(jnp.zeros((NS, columns), jnp.float32), partial_value, (jnp.int32(0), (start * NPA).astype(jnp.int32)))
        return (coeff + placed, None)
    coeff, unused = lax.scan(add_domain, jnp.zeros((NS, columns), jnp.float32), (blocks, proj, offsets))
    table = (species[:, None] == jnp.arange(NSPEC, dtype=jnp.int32)[None, :]).astype(jnp.float32)
    per_atom = jnp.einsum('as,sij->aij', table, augment_q, precision=highest)
    weighted = jnp.einsum('nai,aij->naj', coeff.reshape(NS, NA, NPA), per_atom, precision=highest).reshape(NS, columns)
    gram = product(psi, psi.T) + product(weighted, coeff.T)
    lower = jnp.linalg.cholesky(gram)
    mixing = lax.linalg.triangular_solve(lower, rotation, left_side=True, lower=True, transpose_a=True)
    new_psi = product(mixing.T, psi)
    new_coeff = product(mixing.T, coeff)
    weight = occupation / NS
    density = jnp.sum(weight[:, None] * new_psi * new_psi, axis=0) * NCELLS
    shaped = new_coeff.reshape(NS, NA, NPA)
    rho_ij = jnp.einsum('n,nai,naj->aij', occupation, shaped, shaped, precision=highest).reshape(NA, NPA * NPA)
    return (new_psi, density, rho_ij)
```

```python
import functools
import jax, jax.numpy as jnp
from jax import lax
from jax.experimental import pallas as pl
from jax.experimental.pallas import tpu as pltpu
from jax.sharding import PartitionSpec as P
f32, bf16 = jnp.float32, jnp.bfloat16
NB=8
def split(x):
    hi = x.astype(bf16)
    return hi, (x - hi.astype(f32)).astype(bf16)
def nt(a, b):
    return lax.dot_general(a, b, (((1,),(1,)),((),())), preferred_element_type=f32)
def nn(a, b):
    return jnp.dot(a, b, preferred_element_type=f32)
def dot3(f, a, b):
    return f(a[0], b[0]) + (f(a[0], b[1]) + f(a[1], b[0]))

def lane_b(v, c): return jnp.broadcast_to(v[:, c:c+1], (8,128))
def row_b(v, s): return jnp.broadcast_to(v[s:s+1, :], (8,128))

def diag(V, hook):
    V = list(V)
    row = lax.broadcasted_iota(jnp.int32, (8,128), 0)
    lane = lax.broadcasted_iota(jnp.int32, (8,128), 1)
    Wp = [jnp.where(lane == row + 8*i, 1.0, 0.0).astype(f32) for i in range(16)]
    out = []
    for j in range(16):
        C = {i: [lane_b(V[i], 8*j+t) for t in range(8)] for i in range(j, 16)}
        D = {(s,t): row_b(C[j][t], s) for t in range(8) for s in range(t, 8)}
        RA = [row_b(V[j], t) for t in range(8)]
        RW = [row_b(Wp[j], t) for t in range(8)]
        for t0 in range(0, 8, 2):
            t1 = t0+1
            a, b, c = D[t0,t0], D[t1,t0], D[t1,t1]
            det = a*c - b*b
            r0 = 1.0/a
            rd = 1.0/det
            r1 = a*rd
            for t, r in ((t0,r0),(t1,r1)):
                l = {s: D[s,t]*r for s in range(t+1,8)}
                for s in range(t+1,8):
                    for u in range(t+1,s+1):
                        if s==u==t1 and t==t0: continue
                        D[s,u] = D[s,u] - l[s]*D[u,t]
                for s in range(t+1,8):
                    RA[s] = RA[s] - l[s]*RA[t]
                    RW[s] = RW[s] - l[s]*RW[t]
                for i in range(j+1,16):
                    li = C[i][t]*r
                    for u in range(t+1,8):
                        C[i][u] = C[i][u] - li*D[u,t]
                    V[i] = V[i] - li*RA[t]
                    Wp[i] = Wp[i] - li*RW[t]
            D[t1,t1] = det*r0
        w = RW[0]*lax.rsqrt(D[0,0])
        for t in range(1,8):
            w = jnp.where(row==t, RW[t]*lax.rsqrt(D[t,t]), w)
        out.append(w)
        hook()
    return jnp.concatenate(out, axis=0)

def kern(s_ref, b_ref, y_ref, A, B):
    A[...] = s_ref[...]
    B[...] = b_ref[...]
    pending = []
    def hook():
        if pending: pending.pop(0)()
    for k in range(NB):
        r = pl.ds(128*k, 128)
        W = diag([A[128*k+8*i:128*k+8*i+8, 128*k:128*k+128] for i in range(16)], hook)
        while pending: hook()
        Wp = split(W)
        Bk = split(B[r, :])
        Y = dot3(nn, Wp, Bk)
        y_ref[r, :] = Y
        if k == NB-1: break
        L = dot3(nt, split(A[128*(k+1):, 128*k:128*k+128]), Wp)
        Lp = split(L)
        Yp = split(Y)
        def upd(c, k=k, Lp=Lp):
            o = 128*(c-k-1)
            Lc = tuple(x[o:o+128] for x in Lp)
            Lr = tuple(x[o:] for x in Lp)
            A[128*c:, 128*c:128*c+128] -= dot3(nt, Lr, Lc)
        def updB(i, k=k, Lp=Lp, Yp=Yp):
            o = 128*(i-k-1)
            B[128*i:128*i+128, :] -= dot3(nn, tuple(x[o:o+128] for x in Lp), Yp)
        o=0
        A[128*(k+1):128*(k+2), 128*(k+1):128*(k+2)] -= dot3(nt, tuple(x[:128] for x in Lp), tuple(x[:128] for x in Lp))
        def upd0(k=k, Lp=Lp):
            if k+2 < NB:
                A[128*(k+2):, 128*(k+1):128*(k+2)] -= dot3(nt, tuple(x[128:] for x in Lp), tuple(x[:128] for x in Lp))
        pending.append(upd0)
        for c in range(k+2, NB): pending.append(functools.partial(upd, c))
        for i in range(k+1, NB): pending.append(functools.partial(updB, i))

def cholsolve(s, b):
    n, m = b.shape
    return pl.pallas_call(kern, out_shape=jax.ShapeDtypeStruct((n,m), f32),
        in_specs=[pl.BlockSpec(memory_space=pltpu.VMEM)]*2, out_specs=pl.BlockSpec(memory_space=pltpu.VMEM),
        scratch_shapes=[pltpu.VMEM((n,n), f32), pltpu.VMEM((n,m), f32)],
        compiler_params=pltpu.CompilerParams(vmem_limit_bytes=48*2**20))(s, b)


highest = lax.Precision.HIGHEST


def on_device(psi, proj, offsets, species, augment_q, rotation, occupation):
    states, cells = psi.shape
    groups, doms = lax.axis_size("grp"), lax.axis_size("dom")
    kinds, channels, _ = augment_q.shape
    atoms = species.shape[0]
    total, own_cells, own_atoms = states*groups, cells//groups, atoms//doms
    part = psi.reshape(states, groups, own_cells)
    psi_c = lax.all_to_all(part, "grp", 1, 0, tiled=True).reshape(total, own_cells)
    partial = jnp.dot(psi, proj[0].T, precision=highest)
    placed = lax.dynamic_update_slice(
        jnp.zeros((states, atoms*channels), f32), partial, (jnp.int32(0), offsets[0]*channels))
    mine = lax.psum_scatter(placed, "dom", scatter_dimension=1, tiled=True)
    coeff = lax.all_gather(mine, "grp", axis=0, tiled=True)
    first = lax.axis_index("dom")*own_atoms
    kind = lax.dynamic_slice_in_dim(species, first, own_atoms, 0)
    table = (kind[:, None] == jnp.arange(kinds, dtype=jnp.int32)[None, :]).astype(f32)
    per_atom = jnp.einsum("as,sij->aij", table, augment_q, precision=highest)
    weighted = jnp.einsum("nai,aij->naj", coeff.reshape(total, own_atoms, channels), per_atom, precision=highest)
    weighted = weighted.reshape(total, -1) * (1.0/groups)
    left = jnp.concatenate([psi_c, weighted], axis=1)
    right = jnp.concatenate([psi_c, coeff], axis=1)
    gram = lax.psum(jnp.dot(left, right.T, precision=highest), ("dom", "grp"))
    both = jnp.concatenate([psi_c, coeff, jnp.zeros((total, 256-own_cells-coeff.shape[1]), f32)], axis=1)
    half = cholsolve(gram, both)
    new = jnp.dot(rotation.T, half, precision=highest)
    new_c = new[:, :own_cells]
    density = jnp.sum((occupation/total)[:, None]*new_c*new_c, axis=0)*(cells*doms)
    shaped = new[:, own_cells:own_cells+own_atoms*channels].reshape(total, own_atoms, channels)
    rho = jnp.einsum("n,nai,naj->aij", occupation, shaped, shaped, precision=highest).reshape(own_atoms, channels*channels)
    rho = lax.all_gather(rho, "dom", axis=0, tiled=True)
    back = lax.all_to_all(new_c.reshape(groups, states, own_cells), "grp", 0, 1, tiled=False)
    return back.reshape(states, cells), density, rho


def solution(mesh):
    placed = (P("grp", "dom"), P("dom", None, None), P("dom"), P(), P(), P(), P())
    return jax.shard_map(
        on_device, mesh=mesh, in_specs=placed,
        out_specs=(P("grp", "dom"), P(("dom", "grp")), P()), check_vma=False)
```

```python
import functools
import jax, jax.numpy as jnp
from jax import lax
from jax.experimental import pallas as pl
from jax.experimental.pallas import tpu as pltpu
from jax.sharding import PartitionSpec as P
f32, bf16 = jnp.float32, jnp.bfloat16
NB=8
def split(x):
    hi = x.astype(bf16)
    return hi, (x - hi.astype(f32)).astype(bf16)
def nt(a, b):
    return lax.dot_general(a, b, (((1,),(1,)),((),())), preferred_element_type=f32)
def nn(a, b):
    return jnp.dot(a, b, preferred_element_type=f32)
def dot3(f, a, b):
    return f(a[0], b[0]) + (f(a[0], b[1]) + f(a[1], b[0]))

def lane_b(v, c): return jnp.broadcast_to(v[:, c:c+1], (8,128))
def row_b(v, s): return jnp.broadcast_to(v[s:s+1, :], (8,128))

def diag(V, hook):
    V = list(V)
    row = lax.broadcasted_iota(jnp.int32, (8,128), 0)
    lane = lax.broadcasted_iota(jnp.int32, (8,128), 1)
    Wp = [jnp.where(lane == row + 8*i, 1.0, 0.0).astype(f32) for i in range(16)]
    out = []
    for j in range(16):
        C = {i: [lane_b(V[i], 8*j+t) for t in range(8)] for i in range(j, 16)}
        D = {(s,t): row_b(C[j][t], s) for t in range(8) for s in range(t, 8)}
        RA = [row_b(V[j], t) for t in range(8)]
        RW = [row_b(Wp[j], t) for t in range(8)]
        for t0 in range(0, 8, 2):
            t1 = t0+1
            a, b, c = D[t0,t0], D[t1,t0], D[t1,t1]
            det = a*c - b*b
            r0 = 1.0/a
            rd = 1.0/det
            r1 = a*rd
            for t, r in ((t0,r0),(t1,r1)):
                l = {s: D[s,t]*r for s in range(t+1,8)}
                for s in range(t+1,8):
                    for u in range(t+1,s+1):
                        if s==u==t1 and t==t0: continue
                        D[s,u] = D[s,u] - l[s]*D[u,t]
                for s in range(t+1,8):
                    RA[s] = RA[s] - l[s]*RA[t]
                    RW[s] = RW[s] - l[s]*RW[t]
                for i in range(j+1,16):
                    li = C[i][t]*r
                    for u in range(t+1,8):
                        C[i][u] = C[i][u] - li*D[u,t]
                    V[i] = V[i] - li*RA[t]
                    Wp[i] = Wp[i] - li*RW[t]
            D[t1,t1] = det*r0
        w = RW[0]*lax.rsqrt(D[0,0])
        for t in range(1,8):
            w = jnp.where(row==t, RW[t]*lax.rsqrt(D[t,t]), w)
        out.append(w)
        hook()
    return jnp.concatenate(out, axis=0)

MESH = pl.DeviceIdType.MESH
highest = lax.Precision.HIGHEST
BLK = 128
UNIT = 64
START = [sum(NB - j for j in range(c)) for c in range(NB + 1)]
HALF = START[NB] * UNIT
CHUNKS = 3
CH = HALF // CHUNKS
L1 = CH // 4
L2 = L1 // 8


class Place:
    def __init__(self):
        self.d, self.g = lax.axis_index("dom"), lax.axis_index("grp")
        self.z, self.ylo = self.d // 2, lax.rem(self.d, 2)
        self.yhi, self.x, self.core = self.g // 8, lax.rem(self.g // 2, 4), lax.rem(self.g, 2)
        self.y = self.yhi * 2 + self.ylo
        self.mine = {"x": self.x, "y": self.y, "z": self.z}
        self.size = {"x": 4, "y": 4, "z": 8}

    def at(self, axis, i):
        if axis == "x":
            return {"dom": self.d, "grp": self.yhi * 8 + i * 2 + self.core}
        if axis == "z":
            return {"dom": i * 2 + self.ylo, "grp": self.g}
        return {"dom": self.z * 2 + lax.rem(i, 2), "grp": (i // 2) * 8 + self.x * 2 + self.core}

    def other_core(self):
        return {"dom": self.d, "grp": self.g + 1 - 2 * self.core}


def greet(me, corner):
    barrier = pltpu.get_barrier_semaphore()

    def one(p, carry):
        pl.semaphore_signal(barrier, inc=1, device_id={"dom": me.d, "grp": lax.rem(me.g + p, 16)}, device_id_type=MESH)
        pl.semaphore_signal(barrier, inc=1, device_id={"dom": lax.rem(me.d + p, 16), "grp": me.g}, device_id_type=MESH)
        return carry

    lax.fori_loop(1, 16, one, 0)
    if corner:
        pl.semaphore_signal(barrier, inc=1, device_id=me.at("y", 3 - me.y), device_id_type=MESH)
        pl.semaphore_wait(barrier, 31)
    else:
        pl.semaphore_wait(barrier, 30)


def remote(src, dst, send, recv, device):
    return pltpu.make_async_remote_copy(
        src_ref=src, dst_ref=dst, send_sem=send, recv_sem=recv, device_id=device, device_id_type=MESH)


def rows(first, count, unit):
    return pl.ds(pl.multiple_of(first, unit), count)


def gather_kernel(psi, proj, off, species, aug, o, pc, cf,
                  placed, got, xs, zs, t, rc, h, r1, q1, r2, q2, r3,
                  s_psi, r_psi, s_dom, r_dom, s_cf, r_cf, s_core, r_core, s_x, r_x, s_z, r_z):
    me = Place()
    greet(me, True)
    sends = []
    own = rows(me.g * UNIT, UNIT, UNIT)

    def send_psi(p, carry):
        to = lax.rem(me.g + p, 16)
        remote(psi.at[:, rows(to * BLK, BLK, BLK)], pc.at[own, :], s_psi.at[p], r_psi.at[p],
               {"dom": me.d, "grp": to}).start()
        return carry

    lax.fori_loop(1, 16, send_psi, 0)
    pc[own, :] = psi[:, rows(me.g * BLK, BLK, BLK)]

    value = split(dot3(nt, split(psi[...]), split(proj[0])))
    first = off[0] * 8
    for d in range(16):
        source = lax.broadcasted_iota(jnp.int32, (BLK, BLK), 0) + first
        lane = lax.broadcasted_iota(jnp.int32, (BLK, BLK), 1)
        pick = jnp.where((lane < UNIT) & (source == lane + UNIT * d), 1.0, 0.0).astype(bf16)
        placed[d] = nn(value[0], pick) + nn(value[1], pick)

    def send_dom(p, carry):
        to = lax.rem(me.d + p, 16)
        remote(placed.at[to], got.at[p], s_dom.at[p], r_dom.at[p], {"dom": to, "grp": me.g}).start()
        return carry

    lax.fori_loop(1, 16, send_dom, 0)

    lane = lax.broadcasted_iota(jnp.int32, (8, BLK), 1)
    blocks = [jnp.where(lane // 8 == a, aug[species[me.d * 8 + a]], 0.0) for a in range(8)]
    blocks.append(jnp.zeros((UNIT, BLK), f32))
    q = split(jnp.concatenate(blocks, axis=0) * (1.0 / 16))

    def add_dom(p, total):
        remote(placed.at[0], got.at[p], s_dom.at[p], r_dom.at[p], {"dom": me.d, "grp": me.g}).wait_recv()
        return total + got[p]

    cf[own, :] = lax.fori_loop(1, 16, add_dom, placed[me.d])

    def send_cf(p, carry):
        to = lax.rem(me.g + p, 16)
        remote(cf.at[own, :], cf.at[own, :], s_cf.at[p], r_cf.at[p], {"dom": me.d, "grp": to}).start()
        return carry

    lax.fori_loop(1, 16, send_cf, 0)

    def wait_psi(p, carry):
        remote(psi.at[:, pl.ds(0, BLK)], pc.at[own, :], s_psi.at[p], r_psi.at[p], {"dom": me.d, "grp": me.g}).wait_recv()
        return carry

    def wait_cf(p, carry):
        remote(cf.at[own, :], cf.at[own, :], s_cf.at[p], r_cf.at[p], {"dom": me.d, "grp": me.g}).wait_recv()
        return carry

    lax.fori_loop(1, 16, wait_psi, 0)
    hi, lo = split(pc[...])
    xs[0, :, :BLK] = hi
    xs[1, :, :BLK] = lo
    zs[0, :, :BLK] = hi
    zs[1, :, :BLK] = lo
    lax.fori_loop(1, 16, wait_cf, 0)
    hi, lo = split(cf[...])
    zs[0, :, BLK:] = hi
    zs[1, :, BLK:] = lo
    hi, lo = split(dot3(nn, (hi, lo), q))
    xs[0, :, BLK:] = hi
    xs[1, :, BLK:] = lo

    order = [("x", "y"), ("y", "x"), ("x", "y")]
    started = []

    def go(copy):
        copy.start()
        started.append(copy)
        return copy

    waits = {}

    def start_core(c):
        waits["a", c] = go(remote(t.at[1 - me.core, pl.ds(CH * c, CH)], rc.at[c], s_core.at[c], r_core.at[c], me.other_core()))

    def spread(axis, source, target, s_sem, r_sem):
        n = me.size[axis]
        copies = []
        for p in range(1, n):
            to = lax.rem(me.mine[axis] + p, n)
            copies.append(go(remote(source(to), target(p), s_sem(p), r_sem(p), me.at(axis, to))))
        return copies

    def step_b(c):
        waits["a", c].wait_recv()
        h[c] = t[me.core, pl.ds(CH * c, CH)] + rc[c]
        waits["b", c] = spread(order[c][0], lambda to: h.at[c, rows(to * L1, L1, L1)], lambda p: r1.at[c, p],
                               lambda p: s_x.at[c, 0, p], lambda p: r_x.at[c, 0, p])

    def step_c(c):
        for copy in waits["b", c]:
            copy.wait_recv()
        q1[c] = h[c, rows(me.mine[order[c][0]] * L1, L1, L1)] + r1[c, 1] + r1[c, 2] + r1[c, 3]
        waits["c", c] = spread("z", lambda to: q1.at[c, rows(to * L2, L2, L2)], lambda p: r2.at[c, p],
                               lambda p: s_z.at[c, 0, p], lambda p: r_z.at[c, 0, p])

    def step_d(c):
        for copy in waits["c", c]:
            copy.wait_recv()
        total = q1[c, rows(me.z * L2, L2, L2)]
        for p in range(1, 8):
            total = total + r2[c, p]
        q2[c] = total
        axis = order[c][1]
        waits["d", c] = spread(axis, lambda to: q2.at[c], lambda p: r3.at[c, p],
                               lambda p: s_x.at[c, 1, p], lambda p: r_x.at[c, 1, p])

    def place(c):
        return CH * c + me.mine[order[c][0]] * L1

    def step_e(c):
        for copy in waits["d", c]:
            copy.wait_recv()
        here = o.at[me.core, rows(place(c) + me.z * L2, L2, L2)]
        here[...] = (q2[c] + r3[c, 2]) + (r3[c, 1] + r3[c, 3])
        waits["e", c] = spread("z", lambda to: here, lambda p: here, lambda p: s_z.at[c, 1, p], lambda p: r_z.at[c, 1, p])

    def step_f(c):
        for copy in waits["e", c]:
            copy.wait_recv()
        here = o.at[me.core, rows(place(c), L1, L1)]
        waits["f", c] = spread(order[c][0], lambda to: here, lambda p: here, lambda p: s_x.at[c, 2, p], lambda p: r_x.at[c, 2, p])

    def step_g(c):
        for copy in waits["f", c]:
            copy.wait_recv()
        here = o.at[me.core, pl.ds(CH * c, CH)]
        waits["g", c] = go(remote(here, here, s_core.at[CHUNKS + c], r_core.at[CHUNKS + c], me.other_core()))

    ready = 0
    for c in range(NB):
        block = slice(BLK * c, BLK * c + BLK)
        part = dot3(nt, (xs[0, BLK * c:], xs[1, BLK * c:]), (zs[0, block], zs[1, block]))
        for r in range(NB - c):
            for half in range(2):
                t[half, pl.ds(UNIT * (START[c] + r), UNIT)] = part[BLK * r + UNIT * half: BLK * r + UNIT * half + UNIT]
        while ready < CHUNKS and CH * (ready + 1) <= START[c + 1] * UNIT:
            start_core(ready)
            ready += 1
    for name, c in ("b0", "b1", "b2", "c0", "c1", "d0", "d1", "c2", "e0", "e1", "d2", "f0", "f1", "e2", "g0", "g1", "f2", "g2"):
        {"b": step_b, "c": step_c, "d": step_d, "e": step_e, "f": step_f, "g": step_g}[name](int(c))
    for c in range(CHUNKS):
        waits["g", c].wait_recv()

    def drain(p, carry):
        remote(psi.at[:, pl.ds(0, BLK)], pc.at[own, :], s_psi.at[p], r_psi.at[p], {"dom": me.d, "grp": me.g}).wait_send()
        remote(placed.at[0], got.at[p], s_dom.at[p], r_dom.at[p], {"dom": me.d, "grp": me.g}).wait_send()
        remote(cf.at[own, :], cf.at[own, :], s_cf.at[p], r_cf.at[p], {"dom": me.d, "grp": me.g}).wait_send()
        return carry

    lax.fori_loop(1, 16, drain, 0)
    for copy in started:
        copy.wait_send()


def summed_gram(psi, proj, off, species, aug):
    vm, sm = pl.BlockSpec(memory_space=pltpu.VMEM), pl.BlockSpec(memory_space=pltpu.SMEM)
    total = NB * BLK
    dma = pltpu.SemaphoreType.DMA
    return pl.pallas_call(
        gather_kernel,
        out_shape=(jax.ShapeDtypeStruct((2, HALF, BLK), f32), jax.ShapeDtypeStruct((total, BLK), f32),
                   jax.ShapeDtypeStruct((total, BLK), f32)),
        in_specs=[vm, vm, sm, sm, vm], out_specs=(vm, vm, vm),
        scratch_shapes=[
            pltpu.VMEM((16, UNIT, BLK), f32), pltpu.VMEM((16, UNIT, BLK), f32),
            pltpu.VMEM((2, total, 2 * BLK), bf16), pltpu.VMEM((2, total, 2 * BLK), bf16),
            pltpu.VMEM((2, HALF, BLK), f32), pltpu.VMEM((CHUNKS, CH, BLK), f32), pltpu.VMEM((CHUNKS, CH, BLK), f32),
            pltpu.VMEM((CHUNKS, 4, L1, BLK), f32), pltpu.VMEM((CHUNKS, L1, BLK), f32),
            pltpu.VMEM((CHUNKS, 8, L2, BLK), f32), pltpu.VMEM((CHUNKS, L2, BLK), f32),
            pltpu.VMEM((CHUNKS, 4, L2, BLK), f32),
            dma((16,)), dma((16,)), dma((16,)), dma((16,)), dma((16,)), dma((16,)),
            dma((2 * CHUNKS,)), dma((2 * CHUNKS,)),
            dma((CHUNKS, 3, 4)), dma((CHUNKS, 3, 4)), dma((CHUNKS, 2, 8)), dma((CHUNKS, 2, 8))],
        compiler_params=pltpu.CompilerParams(collective_id=0, has_side_effects=True, vmem_limit_bytes=48 * 2**20),
    )(psi, proj, off, species, aug)


def factor_kernel(o, pc, cf, y_ref, A, B):
    for c in range(NB):
        for r in range(c, NB):
            for half in range(2):
                A[BLK * r + UNIT * half: BLK * r + UNIT * half + UNIT, BLK * c:BLK * c + BLK] = \
                    o[half, UNIT * (START[c] + r - c): UNIT * (START[c] + r - c) + UNIT]
    B[:, :BLK] = pc[...]
    B[:, BLK:] = cf[...]
    pending = []

    def hook():
        if pending:
            pending.pop(0)()

    for k in range(NB):
        r = pl.ds(BLK * k, BLK)
        W = diag([A[BLK * k + 8 * i:BLK * k + 8 * i + 8, BLK * k:BLK * k + BLK] for i in range(16)], hook)
        while pending:
            hook()
        Wp = split(W)
        Y = dot3(nn, Wp, split(B[r, :]))
        y_ref[r, :] = Y
        if k == NB - 1:
            break
        L = dot3(nt, split(A[BLK * (k + 1):, BLK * k:BLK * k + BLK]), Wp)
        Lp, Yp = split(L), split(Y)
        A[BLK * (k + 1):BLK * (k + 2), BLK * (k + 1):BLK * (k + 2)] -= \
            dot3(nt, tuple(v[:BLK] for v in Lp), tuple(v[:BLK] for v in Lp))

        def below(k=k, Lp=Lp):
            if k + 2 < NB:
                A[BLK * (k + 2):, BLK * (k + 1):BLK * (k + 2)] -= \
                    dot3(nt, tuple(v[BLK:] for v in Lp), tuple(v[:BLK] for v in Lp))

        def column(c, k=k, Lp=Lp):
            s = BLK * (c - k - 1)
            A[BLK * c:, BLK * c:BLK * c + BLK] -= \
                dot3(nt, tuple(v[s:] for v in Lp), tuple(v[s:s + BLK] for v in Lp))

        def right(i, k=k, Lp=Lp, Yp=Yp):
            s = BLK * (i - k - 1)
            B[BLK * i:BLK * i + BLK, :] -= dot3(nn, tuple(v[s:s + BLK] for v in Lp), Yp)

        pending.append(below)
        pending.extend(functools.partial(column, c) for c in range(k + 2, NB))
        pending.extend(functools.partial(right, i) for i in range(k + 1, NB))


def factor(o, pc, cf):
    vm = pl.BlockSpec(memory_space=pltpu.VMEM)
    n = NB * BLK
    return pl.pallas_call(
        factor_kernel, out_shape=jax.ShapeDtypeStruct((n, 2 * BLK), f32),
        in_specs=[vm] * 3, out_specs=vm,
        scratch_shapes=[pltpu.VMEM((n, n), f32), pltpu.VMEM((n, 2 * BLK), f32)],
        compiler_params=pltpu.CompilerParams(vmem_limit_bytes=48 * 2**20))(o, pc, cf)


def return_kernel(new, rho, out, all_rho, s_new, r_new, s_rho, r_rho):
    me = Place()
    greet(me, False)
    columns = rows(me.g * BLK, BLK, BLK)
    own = rows(me.d * 8, 8, 8)

    def both(p, to_g, to_d):
        return (remote(new.at[rows(to_g * UNIT, UNIT, UNIT), :], out.at[:, columns], s_new.at[p], r_new.at[p],
                       {"dom": me.d, "grp": to_g}),
                remote(rho, all_rho.at[own, :], s_rho.at[p], r_rho.at[p], {"dom": to_d, "grp": me.g}))

    def send(p, carry):
        for copy in both(p, lax.rem(me.g + p, 16), lax.rem(me.d + p, 16)):
            copy.start()
        return carry

    def wait(p, carry):
        for copy in both(p, lax.rem(me.g + p, 16), lax.rem(me.d + p, 16)):
            copy.wait()
        return carry

    lax.fori_loop(1, 16, send, 0)
    out[:, columns] = new[rows(me.g * UNIT, UNIT, UNIT), :]
    all_rho[own, :] = rho[...]
    lax.fori_loop(1, 16, wait, 0)


def give_back(new, rho):
    vm = pl.BlockSpec(memory_space=pltpu.VMEM)
    dma = pltpu.SemaphoreType.DMA
    return pl.pallas_call(
        return_kernel,
        out_shape=(jax.ShapeDtypeStruct((UNIT, 16 * BLK), f32), jax.ShapeDtypeStruct((BLK, BLK), f32)),
        in_specs=[vm] * 2, out_specs=(vm, vm),
        scratch_shapes=[dma((16,)), dma((16,)), dma((16,)), dma((16,))],
        compiler_params=pltpu.CompilerParams(collective_id=1, has_side_effects=True))(new, rho)


def on_device(psi, proj, offsets, species, augment_q, rotation, occupation):
    states, cells = psi.shape
    groups, doms = lax.axis_size("grp"), lax.axis_size("dom")
    channels = augment_q.shape[1]
    total, own_cells, own_atoms = states * groups, cells // groups, species.shape[0] // doms
    aug = jnp.tile(augment_q, (1, 1, BLK // channels))
    o, psi_c, coeff = summed_gram(psi, proj, offsets, species, aug)
    half = factor(o, psi_c, coeff)
    new = jnp.dot(rotation.T, half, precision=highest)
    new_c = new[:, :own_cells]
    density = jnp.sum((occupation / total)[:, None] * new_c * new_c, axis=0) * (cells * doms)
    shaped = new[:, own_cells:own_cells + own_atoms * channels].reshape(total, own_atoms, channels)
    rho = jnp.einsum("n,nai,naj->aij", occupation, shaped, shaped, precision=highest).reshape(own_atoms, channels * channels)
    rho = jnp.pad(rho, ((0, 0), (0, BLK - channels * channels)))
    new_psi, all_rho = give_back(new_c, rho)
    return new_psi, density, all_rho[:, :channels * channels]


def solution(mesh):
    placed = (P("grp", "dom"), P("dom", None, None), P("dom"), P(), P(), P(), P())
    return jax.shard_map(
        on_device, mesh=mesh, in_specs=placed,
        out_specs=(P("grp", "dom"), P(("dom", "grp")), P()), check_vma=False)
```

```python
import functools
import jax
import jax.numpy as jnp
from jax import lax
from jax.experimental import pallas as pl
from jax.experimental.pallas import tpu as pltpu
from jax.sharding import PartitionSpec as P

f32, bf16 = jnp.float32, jnp.bfloat16
MESH = pl.DeviceIdType.MESH
NB = 8
BLK = 128
TOTAL = NB * BLK
UNIT = 64
START = [sum(NB - j for j in range(c)) for c in range(NB + 1)]
HALF = START[NB] * UNIT
CHUNK = (4, 16, 16)
CH = [u * UNIT for u in CHUNK]
CO = [sum(CH[:c]) for c in range(len(CH) + 1)]
PAD = 10


def split(v):
    hi = v.astype(bf16)
    return hi, (v - hi.astype(f32)).astype(bf16)


def nt(a, b):
    return lax.dot_general(a, b, (((1,), (1,)), ((), ())), preferred_element_type=f32)


def nn(a, b):
    return jnp.dot(a, b, preferred_element_type=f32)


def dot3(f, a, b):
    return f(a[0], b[0]) + (f(a[0], b[1]) + f(a[1], b[0]))


def dot3_nt(a, b):
    high = b[:, :BLK]
    return nt(a, jnp.concatenate([high, high], axis=1)) + nt(a[:, :BLK], b[:, BLK:])


def dot3_nn(a, b):
    return nn(a, jnp.concatenate([b[0], b[0]], axis=0)) + nn(a[:, :BLK], b[1])


def join(v):
    return jnp.concatenate(split(v), axis=1)


def rows(first, count, unit=8):
    return pl.ds(pl.multiple_of(first, unit), count)


class Place:
    def __init__(self):
        self.d, self.g = lax.axis_index("dom"), lax.axis_index("grp")
        self.core, self.chip = lax.rem(self.g, 2), self.g // 2

    def dom(self, i):
        return {"dom": i, "grp": self.g}

    def grp(self, i):
        return {"dom": self.d, "grp": i}

    def other_core(self):
        return self.grp(self.g + 1 - 2 * self.core)


def greet(me):
    barrier = pltpu.get_barrier_semaphore()

    def one(p, carry):
        pl.semaphore_signal(barrier, inc=1, device_id=me.grp(lax.rem(me.g + p, 16)), device_id_type=MESH)
        pl.semaphore_signal(barrier, inc=1, device_id=me.dom(lax.rem(me.d + p, 16)), device_id_type=MESH)
        return carry

    lax.fori_loop(1, 16, one, 0)
    pl.semaphore_wait(barrier, 30)


def remote(src, dst, send, recv, device):
    return pltpu.make_async_remote_copy(
        src_ref=src, dst_ref=dst, send_sem=send, recv_sem=recv, device_id=device, device_id_type=MESH)


def row_b(v, s):
    return jnp.broadcast_to(v[s:s + 1, :], (8, BLK))


def recip(a):
    r = pl.reciprocal(a, approx=True)
    return r * (2.0 - a * r)


def inverse_factor(V, hook):
    row = lax.broadcasted_iota(jnp.int32, (8, BLK), 0)
    where = lax.broadcasted_iota(jnp.int32, (16, 8, BLK), 0) * 8 + lax.broadcasted_iota(jnp.int32, (16, 8, BLK), 1)
    W = jnp.where(lax.broadcasted_iota(jnp.int32, (16, 8, BLK), 2) == where, 1.0, 0.0).astype(f32)
    out = []
    for j in range(16):
        col = [jnp.broadcast_to(V[:, :, 8 * j + t:8 * j + t + 1], V.shape) for t in range(8)]
        D = {(s, t): row_b(col[t][0], s) for t in range(8) for s in range(t, 8)}
        RA = [row_b(V[0], t) for t in range(8)]
        RW = [row_b(W[0], t) for t in range(8)]
        scale = []
        more = j < 15
        if more:
            C = [c[1:] for c in col]
            V, W = V[1:], W[1:]
        for t0 in range(0, 8, 2):
            t1 = t0 + 1
            a, b, c = D[t0, t0], D[t1, t0], D[t1, t1]
            det = a * c - b * b
            r0 = recip(a)
            r1 = a * recip(det)
            D[t1, t1] = det * r0
            scale += [lax.rsqrt(a), lax.rsqrt(D[t1, t1])]
            for t, r in ((t0, r0), (t1, r1)):
                l = {s: D[s, t] * r for s in range(t + 1, 8)}
                for s in range(t + 1, 8):
                    for u in range(t + 1, s + 1):
                        if not (s == t1 and t == t0):
                            D[s, u] = D[s, u] - l[s] * D[u, t]
                for s in range(t + 1, 8):
                    RA[s] = RA[s] - l[s] * RA[t]
                    RW[s] = RW[s] - l[s] * RW[t]
                if more:
                    li = C[t] * r[None]
                    for u in range(t + 1, 8):
                        C[u] = C[u] - li * D[u, t][None]
                    V = V - li * RA[t][None]
                    W = W - li * RW[t][None]
        w = RW[0] * scale[0]
        for t in range(1, 8):
            w = jnp.where(row == t, RW[t] * scale[t], w)
        out.append(w)
        hook()
    return jnp.concatenate(out, axis=0)


def kernel(psi, proj, off, species, aug, rot, occ, out, dens, all_rho,
           psi_v, proj_v, rot_v, rt, placed, got, cp, pc, cf, ps, cs, ws, tiled, t, tp, rc, h, r1, q1, r2, o,
           A, B, L, YH, YL, zp, zc, own_rho,
           s_in, s_psi, r_psi, s_dom, r_dom, s_cf, r_cf, s_core, r_core, s_x, r_x, s_z, r_z, s_new, r_new, s_rho, r_rho):
    me = Place()
    loads = [pltpu.make_async_copy(src, dst, s_in.at[i])
             for i, (src, dst) in enumerate(((psi, psi_v), (proj, proj_v), (rot, rot_v)))]
    for load in loads:
        load.start()
    greet(me)
    own = rows(me.g * UNIT, UNIT)

    def psi_copy(p, to):
        return remote(psi.at[:, rows(to * BLK, BLK, BLK)], pc.at[own, :], s_psi.at[p], r_psi.at[p], me.grp(to))

    def dom_copy(p, to):
        return remote(placed.at[to], got.at[p], s_dom.at[p], r_dom.at[p], me.dom(to))

    def cf_copy(p, to):
        return remote(cp.at[me.g], cp.at[me.g], s_cf.at[p], r_cf.at[p], me.grp(to))

    def each(body):
        def one(p, carry):
            body(p)
            return carry
        lax.fori_loop(1, 16, one, 0)

    each(lambda p: psi_copy(p, lax.rem(me.g + p, 16)).start())

    loads[0].wait()
    loads[1].wait()
    pc[own, :] = psi_v[:, rows(me.g * BLK, BLK, BLK)]
    value = dot3(nt, split(psi_v[...]), split(proj_v[0]))
    value = split(jnp.concatenate([value[:32], value[32:]], axis=1))
    source = lax.broadcasted_iota(jnp.int32, (2 * BLK, BLK), 0)
    lane = lax.broadcasted_iota(jnp.int32, (2 * BLK, BLK), 1)
    gap = jnp.where((source < BLK) == (lane < UNIT), lax.rem(source, BLK) - lax.rem(lane, UNIT), -4096) + off[0] * 8
    for d in range(16):
        pick = jnp.where(gap == UNIT * d, 1.0, 0.0).astype(bf16)
        placed[d] = nn(value[0], pick) + nn(value[1], pick)
    each(lambda p: dom_copy(p, lax.rem(me.d + p, 16)).start())

    A[...] = jnp.zeros(A.shape, f32)
    B[pl.ds(TOTAL, (PAD - NB) * BLK), :] = jnp.zeros(((PAD - NB) * BLK, 2 * BLK), f32)
    lane = lax.broadcasted_iota(jnp.int32, (8, BLK), 1)
    repeat = jnp.where(lax.broadcasted_iota(jnp.int32, (8, BLK), 0) == lax.rem(lane, 8), 1.0, 0.0)
    tiled[...] = jnp.dot(aug[...].reshape(32, 8), repeat, precision=lax.Precision.HIGHEST).reshape(4, 8, BLK)
    blocks = [jnp.where(lane // 8 == a, tiled[species[me.d * 8 + a]], 0.0) for a in range(8)]
    blocks.append(jnp.zeros((UNIT, BLK), f32))
    q = split(jnp.concatenate(blocks, axis=0))
    loads[2].wait()

    def turn(i, carry):
        hi, lo = split(rot_v[rows(i * BLK, BLK, BLK), :].T)
        rt[0, :, rows(i * BLK, BLK, BLK)] = hi
        rt[1, :, rows(i * BLK, BLK, BLK)] = lo
        return carry

    lax.fori_loop(0, NB, turn, 0)

    def add_dom(p, total):
        dom_copy(p, me.d).wait_recv()
        return total + got[p]

    started = []
    waits = {}

    def go(copy):
        copy.start()
        started.append(copy)
        return copy

    def arrive(key):
        for copy in waits[key]:
            copy.wait_recv()

    def spread(n, mine, device, source, target, s_sem, r_sem):
        copies = []
        for p in range(1, n):
            to = lax.rem(mine + p, n)
            copies.append(go(remote(source(to), target, s_sem.at[p], r_sem.at[p], device(to))))
        return copies

    def chips(c, i, source, target):
        return spread(8, me.chip, lambda to: me.grp(to * 2 + me.core), source, target, s_x.at[c, i], r_x.at[c, i])

    def doms(c, i, source, target):
        return spread(16, me.d, me.dom, source, target, s_z.at[c, i], r_z.at[c, i])

    def sizes(c):
        return CO[c], CH[c], CO[c] // 8, CH[c] // 8

    def step_a(c):
        chunk = pl.ds(CO[c], CH[c])
        waits["a", c] = [go(remote(t.at[1 - me.core, chunk], rc.at[chunk], s_core.at[c], r_core.at[c], me.other_core()))]

    def step_b(c):
        arrive(("a", c))
        first, count, at, n = sizes(c)
        chunk = pl.ds(first, count)
        h[chunk] = t[me.core, chunk] + rc[chunk]
        waits["b", c] = chips(c, 0, lambda to: h.at[rows(first + to * n, n)], r1.at[me.chip, pl.ds(at, n)])

    def step_c(c):
        arrive(("b", c))
        first, count, at, n = sizes(c)
        mine, part = rows(first + me.chip * n, n), pl.ds(at, n)
        r1[me.chip, part] = h[mine] + tp[mine]
        total = r1[0, part]
        for i in range(1, 8):
            total = total + r1[i, part]
        if c == 0:
            r2[me.d, part] = total
            waits["c", c] = doms(c, 0, lambda to: r2.at[me.d, part], r2.at[me.d, part])
        else:
            q1[part] = total
            m = n // 16
            waits["c", c] = doms(c, 0, lambda to: q1.at[rows(at + to * m, m)], r2.at[me.d, pl.ds(at, m)])

    def step_d(c):
        arrive(("c", c))
        first, count, at, n = sizes(c)
        if c == 0:
            part, here = pl.ds(at, n), o.at[me.core, rows(first + me.chip * n, n)]
        else:
            m = n // 16
            part, here = pl.ds(at, m), o.at[me.core, rows(first + me.chip * n + me.d * m, m)]
            r2[me.d, part] = q1[rows(at + me.d * m, m)]
        total = r2[0, part]
        for i in range(1, 16):
            total = total + r2[i, part]
        here[...] = total
        if c:
            waits["d", c] = doms(c, 1, lambda to: here, here)

    def step_e(c):
        if c:
            arrive(("d", c))
        first, count, at, n = sizes(c)
        here = o.at[me.core, rows(first + me.chip * n, n)]
        waits["e", c] = chips(c, 1, lambda to: here, here)

    def step_f(c):
        arrive(("e", c))
        here = o.at[me.core, pl.ds(CO[c], CH[c])]
        n = len(CHUNK) + c
        waits["f", c] = [go(remote(here, here, s_core.at[n], r_core.at[n], me.other_core()))]

    def step_g(c):
        arrive(("f", c))
        for col in range(NB):
            for r in range(NB - col):
                unit = START[col] + r
                if CO[c] <= unit * UNIT < CO[c + 1]:
                    for half in range(2):
                        A[col, BLK * r + UNIT * half:BLK * r + UNIT * half + UNIT] += o[half, pl.ds(unit * UNIT, UNIT)]

    def do(*names):
        for name in names:
            {"a": step_a, "b": step_b, "c": step_c, "d": step_d, "e": step_e, "f": step_f, "g": step_g}[name[0]](int(name[1]))

    def gram_of_psi():
        ready = 0
        for c in range(NB):
            part = dot3_nt(ps[BLK * c:], ps[BLK * c:BLK * c + BLK])
            for r in range(NB - c):
                for half in range(2):
                    t[half, pl.ds(UNIT * (START[c] + r), UNIT)] = part[BLK * r + UNIT * half: BLK * r + UNIT * half + UNIT]
            while ready < len(CHUNK) and CO[ready + 1] <= START[c + 1] * UNIT:
                step_a(ready)
                ready += 1

    cp[me.g] = lax.fori_loop(1, 16, add_dom, placed[me.d])
    each(lambda p: cf_copy(p, lax.rem(me.g + p, 16)).start())

    each(lambda p: psi_copy(p, me.g).wait_recv())
    ps[...] = join(pc[...])
    gram_of_psi()
    do("b0", "b1")
    B[:TOTAL, :BLK] = pc[...]

    each(lambda p: cf_copy(p, me.g).wait_recv())
    left = lax.broadcasted_iota(jnp.int32, (32, BLK), 1) < UNIT
    for g in range(16):
        cf[UNIT * g:UNIT * g + 32] = jnp.where(left, cp[g], 0.0)
        cf[UNIT * g + 32:UNIT * g + 64] = jnp.where(left, pltpu.roll(cp[g], UNIT, 1), 0.0)
    cs[...] = join(cf[...])
    ws[...] = join(dot3(nn, split(cf[...]), q)).reshape(NB, 2, UNIT, 2 * BLK)
    for c in range(NB):
        own_rows = ws[c:, me.core].reshape((NB - c) * UNIT, 2 * BLK)
        tp[pl.ds(START[c] * UNIT, (NB - c) * UNIT)] = dot3_nt(own_rows, cs[BLK * c:BLK * c + BLK])
    do("c0", "b2")
    B[:TOTAL, BLK:] = cf[...]
    do("c1", "d0", "e0", "c2", "d1", "f0", "d2", "e1", "g0")

    def add_new(i, k):
        piece, past = pl.ds(2 * BLK * i, 2 * BLK), rows(k * BLK, BLK, BLK)
        new = dot3_nn(jnp.concatenate([rt[0, piece, past], rt[1, piece, past]], axis=1), (YH[...], YL[...]))
        zp[piece] += new[:, :BLK]
        zc[piece] += new[:, BLK:]

    def step(k, m, first=False, extra=None, last=()):
        work = []

        def column(b):
            n = max(m - b, 0) if b else m - 1
            a = b if b else 1
            A[k + b, pl.ds(BLK * (a - b), BLK * n), :] -= dot3_nt(L[pl.ds(BLK * a, BLK * n), :], L[pl.ds(BLK * b, BLK), :])

        def right(a):
            B[rows((k + a) * BLK, BLK), :] -= dot3_nn(L[pl.ds(BLK * a, BLK), :], (YH[...], YL[...]))

        if not first:
            work.append(functools.partial(column, 0))
            work.append(functools.partial(right, 0))
            work += [functools.partial(column, b) for b in range(1, m)]
            work += [functools.partial(right, a) for a in range(1, m)]
            work += [functools.partial(add_new, i, k - 1) for i in range(4)]
        total = len(work)
        at = [0]

        def hook():
            at[0] += 1
            if extra and at[0] in extra:
                do(*extra[at[0]])
            while work and total - len(work) < -(-total * at[0] // 15):
                work.pop(0)()

        W = join(inverse_factor(A[k, pl.ds(0, BLK), :].reshape(16, 8, BLK), hook))
        while work:
            work.pop(0)()
        if last:
            do(*last)
        here = rows(k * BLK, BLK)
        hi, lo = split(dot3_nn(W, split(B[here, :])))
        YH[...] = hi
        YL[...] = lo
        if m > 1:
            panel = join(dot3_nt(join(A[k, pl.ds(BLK, BLK * (m - 1)), :]), W))
            L[pl.ds(0, BLK * (m - 1)), :] = panel
            A[k + 1, pl.ds(0, BLK), :] -= dot3_nt(panel[:BLK], panel[:BLK])

    zp[...] = jnp.zeros(zp.shape, f32)
    zc[...] = jnp.zeros(zc.shape, f32)
    step(0, 8, first=True, extra={8: ("e2",)}, last=("f1", "g1"))
    step(1, 7, extra={8: ("f2",)}, last=("g2",))

    def six(k, carry):
        step(k, 6)
        return carry

    def three(k, carry):
        step(k, 3)
        return carry

    lax.fori_loop(2, 5, six, 0)
    lax.fori_loop(5, 8, three, 0)
    for i in range(4):
        add_new(i, NB - 1)

    columns = rows(me.g * BLK, BLK, BLK)

    def new_copy(p, to):
        return remote(zp.at[rows(to * UNIT, UNIT), :], out.at[:, columns], s_new.at[p], r_new.at[p], me.grp(to))

    each(lambda p: new_copy(p, lax.rem(me.g + p, 16)).start())
    out[:, columns] = zp[rows(me.g * UNIT, UNIT), :]

    new = zc[...]
    pair = dot3(nn, split(new.T * occ[...]), split(new))
    r = lax.broadcasted_iota(jnp.int32, (BLK, BLK), 0)
    c = lax.broadcasted_iota(jnp.int32, (BLK, BLK), 1)
    pair = jnp.where(r // 8 == c // 8, pair, 0.0)
    fold = jnp.where((lax.rem(r, 8) == lax.rem(c, 8)) & (c < UNIT), 1.0, 0.0).astype(bf16)
    hi, lo = split(pair)
    pair = jnp.where(lax.rem(r, 8) == c // 8, nn(hi, fold) + nn(lo, fold), 0.0)
    hi, lo = split(pair)
    atom = jnp.where(r[:8] == c[:8] // 8, 1.0, 0.0).astype(bf16)
    own_rho[...] = nn(atom, hi) + nn(atom, lo)
    mine = rows(me.d * 8, 8)

    def rho_copy(p, to):
        return remote(own_rho, all_rho.at[mine, :], s_rho.at[p], r_rho.at[p], me.dom(to))

    each(lambda p: rho_copy(p, lax.rem(me.d + p, 16)).start())
    all_rho[mine, :] = own_rho[...]
    weight = jnp.broadcast_to(occ[...] * (32768.0 / TOTAL), (8, TOTAL))
    dens[...] = dot3(nn, split(weight), split(zp[...] * zp[...]))[:1]

    def drain(p):
        psi_copy(p, me.g).wait_send()
        dom_copy(p, me.d).wait_send()
        cf_copy(p, me.g).wait_send()
        new_copy(p, me.g).wait()
        rho_copy(p, me.d).wait()

    each(drain)
    for copy in started:
        copy.wait_send()


def on_device(psi, proj, offsets, species, augment_q, rotation, occupation):
    states, cells = psi.shape
    channels = augment_q.shape[1]
    vm, sm, hbm = (pl.BlockSpec(memory_space=s) for s in (pltpu.VMEM, pltpu.SMEM, pl.ANY))
    dma, n = pltpu.SemaphoreType.DMA, len(CHUNK)
    sixteen = [dma((16,)), dma((16,))]
    new_psi, density, rho = pl.pallas_call(
        kernel,
        out_shape=(jax.ShapeDtypeStruct((states, cells), f32), jax.ShapeDtypeStruct((1, BLK), f32),
                   jax.ShapeDtypeStruct((BLK, BLK), f32)),
        in_specs=[hbm, hbm, sm, sm, vm, hbm, vm], out_specs=(vm, vm, vm),
        scratch_shapes=[
            pltpu.VMEM(psi.shape, f32), pltpu.VMEM(proj.shape, f32), pltpu.VMEM(rotation.shape, f32),
            pltpu.VMEM((2, TOTAL, TOTAL), bf16),
            pltpu.VMEM((16, 32, BLK), f32), pltpu.VMEM((16, 32, BLK), f32), pltpu.VMEM((16, 32, BLK), f32),
            pltpu.VMEM((TOTAL, BLK), f32), pltpu.VMEM((TOTAL, BLK), f32),
            pltpu.VMEM((TOTAL, 2 * BLK), bf16), pltpu.VMEM((TOTAL, 2 * BLK), bf16), pltpu.VMEM((NB, 2, UNIT, 2 * BLK), bf16),
            pltpu.VMEM((4, 8, BLK), f32),
            pltpu.VMEM((2, HALF, BLK), f32), pltpu.VMEM((HALF, BLK), f32), pltpu.VMEM((HALF, BLK), f32), pltpu.VMEM((HALF, BLK), f32),
            pltpu.VMEM((8, HALF // 8, BLK), f32), pltpu.VMEM((HALF // 8, BLK), f32),
            pltpu.VMEM((16, HALF // 8, BLK), f32), pltpu.VMEM((2, HALF, BLK), f32),
            pltpu.VMEM((PAD, TOTAL, BLK), f32), pltpu.VMEM((PAD * BLK, 2 * BLK), f32),
            pltpu.VMEM((TOTAL, 2 * BLK), bf16),
            pltpu.VMEM((BLK, 2 * BLK), bf16), pltpu.VMEM((BLK, 2 * BLK), bf16),
            pltpu.VMEM((TOTAL, BLK), f32), pltpu.VMEM((TOTAL, BLK), f32),
            pltpu.VMEM((8, BLK), f32),
            dma((3,)), *sixteen, *sixteen, *sixteen,
            dma((2 * n,)), dma((2 * n,)), dma((n, 2, 8)), dma((n, 2, 8)), dma((n, 2, 16)), dma((n, 2, 16)),
            *sixteen, *sixteen],
        compiler_params=pltpu.CompilerParams(collective_id=0, has_side_effects=True, vmem_limit_bytes=56 * 2**20),
    )(psi, proj, offsets, species, augment_q, rotation, occupation.reshape(1, TOTAL))
    return new_psi, density.reshape(BLK), rho[:, :channels * channels]


def solution(mesh):
    placed = (P("grp", "dom"), P("dom", None, None), P("dom"), P(), P(), P(), P())
    return jax.shard_map(
        on_device, mesh=mesh, in_specs=placed,
        out_specs=(P("grp", "dom"), P(("dom", "grp")), P()), check_vma=False)
```

```python
import functools
import jax
import jax.numpy as jnp
from jax import lax
from jax.experimental import pallas as pl
from jax.experimental.pallas import tpu as pltpu
from jax.sharding import PartitionSpec as P

f32, bf16 = jnp.float32, jnp.bfloat16
MESH = pl.DeviceIdType.MESH
NB = 8
BLK = 128
TOTAL = NB * BLK
UNIT = 64
START = [sum(NB - j for j in range(c)) for c in range(NB + 1)]
CHUNK = (8, 8, 8, 8, 8)
HALF = sum(CHUNK) * UNIT
CH = [u * UNIT for u in CHUNK]
CO = [sum(CH[:c]) for c in range(len(CH) + 1)]
NEAR = 4
PAD = 11


def split(v):
    hi = v.astype(bf16)
    return hi, (v - hi.astype(f32)).astype(bf16)


def nt(a, b):
    return lax.dot_general(a, b, (((1,), (1,)), ((), ())), preferred_element_type=f32)


def nn(a, b):
    return jnp.dot(a, b, preferred_element_type=f32)


def dot3(f, a, b):
    return f(a[0], b[0]) + (f(a[0], b[1]) + f(a[1], b[0]))


def dot3_nt(a, b):
    high = b[:, :BLK]
    return nt(a, jnp.concatenate([high, high], axis=1)) + nt(a[:, :BLK], b[:, BLK:])


def dot3_nn(a, b):
    return nn(a, jnp.concatenate([b[0], b[0]], axis=0)) + nn(a[:, :BLK], b[1])


def join(v):
    return jnp.concatenate(split(v), axis=1)


def rows(first, count, unit=8):
    return pl.ds(pl.multiple_of(first, unit), count)


class Place:
    def __init__(self):
        self.d, self.g = lax.axis_index("dom"), lax.axis_index("grp")
        self.core, self.chip = lax.rem(self.g, 2), self.g // 2
        self.z, self.ylo = self.d // 2, lax.rem(self.d, 2)

    def dom(self, i):
        return {"dom": i, "grp": self.g}

    def grp(self, i):
        return {"dom": self.d, "grp": i}

    def other_core(self):
        return self.grp(self.g + 1 - 2 * self.core)


def greet(me):
    barrier = pltpu.get_barrier_semaphore()

    def one(p, carry):
        pl.semaphore_signal(barrier, inc=1, device_id=me.grp(lax.rem(me.g + p, 16)), device_id_type=MESH)
        pl.semaphore_signal(barrier, inc=1, device_id=me.dom(lax.rem(me.d + p, 16)), device_id_type=MESH)
        return carry

    lax.fori_loop(1, 16, one, 0)
    return lambda: pl.semaphore_wait(barrier, 30)


def remote(src, dst, send, recv, device):
    return pltpu.make_async_remote_copy(
        src_ref=src, dst_ref=dst, send_sem=send, recv_sem=recv, device_id=device, device_id_type=MESH)


def row_b(v, s):
    return jnp.broadcast_to(v[s:s + 1, :], (8, BLK))


def recip(a):
    return pltpu.reciprocal(a, approx=True)


def inverse_factor(V, hook):
    row = lax.broadcasted_iota(jnp.int32, (8, BLK), 0)
    lane = lax.broadcasted_iota(jnp.int32, (8, BLK), 1)
    out = []
    for j in range(16):
        n = min(NEAR, 15 - j)
        col = [jnp.broadcast_to(V[:n + 1, :, 8 * j + t:8 * j + t + 1], (n + 1, 8, BLK)) for t in range(8)]
        D = {(s, t): row_b(col[t][0], s) for t in range(8) for s in range(t, 8)}
        here = lane // 8 == j
        first = jnp.where(here, jnp.where(lane == row + 8 * j, 1.0, 0.0), V[0])
        R = [row_b(first, t) for t in range(8)]
        if n:
            C = [c[1:] for c in col]
            V = jnp.where(here[None], 0.0, V[1:])
            N, F = V[:n], V[n:]
        scale = []
        f = [recip(D[t, t]) for t in range(1, 8, 2)]
        for t0 in range(0, 8, 2):
            t1 = t0 + 1
            a, b, c = D[t0, t0], D[t1, t0], D[t1, t1]
            size = f[t0 // 2]
            det = a * (c * size) - b * (b * size)
            r0 = recip(a)
            r1 = (a * size) * recip(det)
            D[t1, t1] = c - (b * r0) * b
            scale += [lax.rsqrt(a), lax.rsqrt(D[t1, t1])]
            for t, r in ((t0, r0), (t1, r1)):
                l = {s: D[s, t] * r for s in range(t + 1, 8)}
                for s in range(t + 1, 8):
                    for u in range(t + 1, s + 1):
                        if not (s == t1 and t == t0):
                            D[s, u] = D[s, u] - l[s] * D[u, t]
                for s in range(t + 1, 8):
                    R[s] = R[s] - l[s] * R[t]
                if n:
                    li = C[t] * r[None]
                    for u in range(t + 1, 8):
                        C[u] = C[u] - li * D[u, t][None]
                    N = N - li * R[t][None]
        w = R[0] * scale[0]
        for t in range(1, 8):
            w = jnp.where(row == t, R[t] * scale[t], w)
        out.append(jnp.where(lane < 8 * j + 8, w, 0.0))
        if n < 15 - j:
            hi = w.astype(bf16).astype(f32)
            lo = w - hi
            left = jnp.concatenate([hi, hi, lo], axis=0).T[8 * (j + 1 + n):].astype(bf16)
            right = jnp.concatenate([hi, lo, hi], axis=0).astype(bf16)
            F = F - nn(left, right).reshape(15 - j - n, 8, BLK)
            V = jnp.concatenate([N, F], axis=0)
        elif n:
            V = N
        hook()
    return jnp.concatenate(out, axis=0)


def kernel(psi, proj, off, species, aug, rot, occ, out, dens, all_rho,
           psi_v, proj_v, rot_v, rt, placed, got, cp, pc, cf, ps, cs, ws, tiled, t, tp, rc, h, r1, q1, r2, q2, r3, o,
           A, B, L, WJ, YH, YL, zp, zc, own_rho,
           s_in, s_psi, r_psi, s_dom, r_dom, s_cf, r_cf, s_core, r_core, s_x, r_x, s_z, r_z, s_y, r_y, s_new, r_new, s_rho, r_rho):
    me = Place()
    loads = [pltpu.make_async_copy(src, dst, s_in.at[i])
             for i, (src, dst) in enumerate(((psi, psi_v), (proj, proj_v), (rot, rot_v)))]
    for load in loads:
        load.start()
    met = greet(me)
    own = rows(me.g * UNIT, UNIT)

    def psi_copy(p, to):
        return remote(psi.at[:, rows(to * BLK, BLK, BLK)], pc.at[own, :], s_psi.at[p], r_psi.at[p], me.grp(to))

    def dom_copy(p, to):
        return remote(placed.at[to], got.at[p], s_dom.at[p], r_dom.at[p], me.dom(to))

    def cf_copy(p, to):
        return remote(cp.at[me.g], cp.at[me.g], s_cf.at[p], r_cf.at[p], me.grp(to))

    def each(body):
        def one(p, carry):
            body(p)
            return carry
        lax.fori_loop(1, 16, one, 0)

    loads[0].wait()
    loads[1].wait()
    pc[own, :] = psi_v[:, rows(me.g * BLK, BLK, BLK)]
    value = dot3(nt, split(psi_v[...]), split(proj_v[0]))
    value = split(jnp.concatenate([value[:32], value[32:]], axis=1))
    source = lax.broadcasted_iota(jnp.int32, (2 * BLK, BLK), 0)
    lane = lax.broadcasted_iota(jnp.int32, (2 * BLK, BLK), 1)
    gap = jnp.where((source < BLK) == (lane < UNIT), lax.rem(source, BLK) - lax.rem(lane, UNIT), -4096) + off[0] * 8
    for d in range(16):
        pick = jnp.where(gap == UNIT * d, 1.0, 0.0).astype(bf16)
        placed[d] = nn(value[0], pick) + nn(value[1], pick)
    met()
    each(lambda p: dom_copy(p, lax.rem(me.d + p, 16)).start())
    each(lambda p: psi_copy(p, lax.rem(me.g + p, 16)).start())

    A[...] = jnp.zeros(A.shape, f32)
    B[pl.ds(TOTAL, (PAD - NB) * BLK), :] = jnp.zeros(((PAD - NB) * BLK, 2 * BLK), f32)
    lane = lax.broadcasted_iota(jnp.int32, (8, BLK), 1)
    repeat = jnp.where(lax.broadcasted_iota(jnp.int32, (8, BLK), 0) == lax.rem(lane, 8), 1.0, 0.0)
    tiled[...] = jnp.dot(aug[...].reshape(32, 8), repeat, precision=lax.Precision.HIGHEST).reshape(4, 8, BLK)
    blocks = [jnp.where(lane // 8 == a, tiled[species[me.d * 8 + a]], 0.0) for a in range(8)]
    blocks.append(jnp.zeros((UNIT, BLK), f32))
    q = split(jnp.concatenate(blocks, axis=0))
    loads[2].wait()

    def turn(i, carry):
        hi, lo = split(rot_v[rows(i * BLK, BLK, BLK), :].T)
        rt[0, :, rows(i * BLK, BLK, BLK)] = hi
        rt[1, :, rows(i * BLK, BLK, BLK)] = lo
        return carry

    lax.fori_loop(0, NB, turn, 0)

    def add_dom(p, total):
        dom_copy(p, me.d).wait_recv()
        return total + got[p]

    started = []
    waits = {}

    def go(copy):
        copy.start()
        started.append(copy)
        return copy

    def arrive(key):
        for copy in waits[key]:
            copy.wait_recv()

    def spread(n, mine, device, source, target, s_sem, r_sem):
        copies = []
        for p in range(1, n):
            to = lax.rem(mine + p, n)
            copies.append(go(remote(source(to), target, s_sem.at[p], r_sem.at[p], device(to))))
        return copies

    def chips(c, i, source, target):
        return spread(8, me.chip, lambda to: me.grp(to * 2 + me.core), source, target, s_x.at[c, i], r_x.at[c, i])

    def along_z(c, i, source, target):
        return spread(8, me.z, lambda to: me.dom(to * 2 + me.ylo), source, target, s_z.at[c, i], r_z.at[c, i])

    def sizes(c):
        return CO[c], CH[c], CO[c] // 8, CH[c] // 8

    def step_a(c):
        chunk = pl.ds(CO[c], CH[c])
        waits["a", c] = [go(remote(t.at[1 - me.core, chunk], rc.at[chunk], s_core.at[c], r_core.at[c], me.other_core()))]

    def step_b(c):
        arrive(("a", c))
        first, count, at, n = sizes(c)
        chunk = pl.ds(first, count)
        h[chunk] = t[me.core, chunk] + rc[chunk]
        waits["b", c] = chips(c, 0, lambda to: h.at[rows(first + to * n, n)], r1.at[me.chip, pl.ds(at, n)])

    def step_c(c):
        arrive(("b", c))
        first, count, at, n = sizes(c)
        mine, part = rows(first + me.chip * n, n), pl.ds(at, n)
        r1[me.chip, part] = h[mine] + tp[mine]
        total = r1[0, part]
        for i in range(1, 8):
            total = total + r1[i, part]
        q1[part] = total
        m = n // 8
        waits["c", c] = along_z(c, 0, lambda to: q1.at[rows(at + to * m, m)], r2.at[me.z, pl.ds(at, m)])

    def step_d(c):
        arrive(("c", c))
        first, count, at, n = sizes(c)
        m = n // 8
        part = pl.ds(at, m)
        r2[me.z, part] = q1[rows(at + me.z * m, m)]
        total = r2[0, part]
        for i in range(1, 8):
            total = total + r2[i, part]
        q2[part] = total
        waits["d", c] = [go(remote(q2.at[part], r3.at[part], s_y.at[c], r_y.at[c], me.dom(me.d + 1 - 2 * me.ylo)))]

    def step_e(c):
        arrive(("d", c))
        first, count, at, n = sizes(c)
        m = n // 8
        here = o.at[me.core, rows(first + me.chip * n + me.z * m, m)]
        here[...] = q2[pl.ds(at, m)] + r3[pl.ds(at, m)]
        waits["e", c] = along_z(c, 1, lambda to: here, here)

    def step_f(c):
        arrive(("e", c))
        first, count, at, n = sizes(c)
        here = o.at[me.core, rows(first + me.chip * n, n)]
        waits["f", c] = chips(c, 1, lambda to: here, here)

    def step_g(c):
        arrive(("f", c))
        here = o.at[me.core, pl.ds(CO[c], CH[c])]
        n = len(CHUNK) + c
        waits["g", c] = [go(remote(here, here, s_core.at[n], r_core.at[n], me.other_core()))]

    def step_h(c):
        arrive(("g", c))
        for col in range(NB):
            for r in range(NB - col):
                unit = START[col] + r
                if CO[c] <= unit * UNIT < CO[c + 1]:
                    for half in range(2):
                        A[col, BLK * r + UNIT * half:BLK * r + UNIT * half + UNIT] += o[half, pl.ds(unit * UNIT, UNIT)]

    def do(*names):
        for name in names:
            {"a": step_a, "b": step_b, "c": step_c, "d": step_d, "e": step_e, "f": step_f, "g": step_g, "h": step_h}[name[0]](int(name[1]))

    def gram_of_psi():
        ready = 0
        padding = pl.ds(START[NB] * UNIT, HALF - START[NB] * UNIT)
        t[:, padding] = jnp.zeros((2, HALF - START[NB] * UNIT, BLK), f32)
        tp[padding] = jnp.zeros((HALF - START[NB] * UNIT, BLK), f32)
        for c in range(NB):
            part = dot3_nt(ps[BLK * c:], ps[BLK * c:BLK * c + BLK])
            for r in range(NB - c):
                for half in range(2):
                    t[half, pl.ds(UNIT * (START[c] + r), UNIT)] = part[BLK * r + UNIT * half: BLK * r + UNIT * half + UNIT]
            while ready < len(CHUNK) and (CO[ready + 1] <= START[c + 1] * UNIT or c == NB - 1):
                step_a(ready)
                ready += 1

    cp[me.g] = lax.fori_loop(1, 16, add_dom, placed[me.d])
    each(lambda p: cf_copy(p, lax.rem(me.g + p, 16)).start())

    each(lambda p: psi_copy(p, me.g).wait_recv())
    ps[...] = join(pc[...])
    gram_of_psi()
    do("b0", "b1", "b2", "b3", "b4")
    B[:TOTAL, :BLK] = pc[...]

    each(lambda p: cf_copy(p, me.g).wait_recv())
    left = lax.broadcasted_iota(jnp.int32, (32, BLK), 1) < UNIT
    for g in range(16):
        cf[UNIT * g:UNIT * g + 32] = jnp.where(left, cp[g], 0.0)
        cf[UNIT * g + 32:UNIT * g + 64] = jnp.where(left, pltpu.roll(cp[g], UNIT, 1), 0.0)
    cs[...] = join(cf[...])
    ws[...] = join(dot3(nn, split(cf[...]), q)).reshape(NB, 2, UNIT, 2 * BLK)
    for c in range(NB):
        own_rows = ws[c:, me.core].reshape((NB - c) * UNIT, 2 * BLK)
        tp[pl.ds(START[c] * UNIT, (NB - c) * UNIT)] = dot3_nt(own_rows, cs[BLK * c:BLK * c + BLK])
    do("c0", "c1")
    B[:TOTAL, BLK:] = cf[...]
    do("c2", "d0", "c3", "d1", "e0", "e1", "d2", "c4", "e2", "f0", "d3", "f1", "e3", "d4", "f2", "g0", "h0")

    def add_new(i, k):
        piece, past = pl.ds(2 * BLK * i, 2 * BLK), rows(k * BLK, BLK, BLK)
        new = dot3_nn(jnp.concatenate([rt[0, piece, past], rt[1, piece, past]], axis=1), (YH[...], YL[...]))
        zp[piece] += new[:, :BLK]
        zc[piece] += new[:, BLK:]

    def finish(k, m):
        def panel(a, n):
            past = A[k, pl.ds(BLK * (a + 1), BLK * n), :]
            L[pl.ds(BLK * a, BLK * n), :] = join(dot3_nt(join(past), WJ[...]))

        def substitute():
            hi, lo = split(dot3_nn(WJ[...], split(B[rows(k * BLK, BLK), :])))
            YH[...] = hi
            YL[...] = lo

        return [functools.partial(panel, a, min(2, m - a)) for a in range(1, m, 2)], substitute

    def step(k, m, first=False, extra=None, last=()):
        work = []

        def column(b):
            n = m - b if b else m - 1
            a = b if b else 1
            A[k + b, pl.ds(BLK * (a - b), BLK * n), :] -= dot3_nt(L[pl.ds(BLK * a, BLK * n), :], L[pl.ds(BLK * b, BLK), :])

        def right(a):
            B[rows((k + a) * BLK, BLK), :] -= dot3_nn(L[pl.ds(BLK * a, BLK), :], (YH[...], YL[...]))

        if not first:
            panels, substitute = finish(k - 1, m)
            work += panels
            work.append(functools.partial(column, 0))
            work.append(substitute)
            work.append(functools.partial(right, 0))
            work += [functools.partial(column, b) for b in range(1, m)]
            work += [functools.partial(right, a) for a in range(1, m)]
            work += [functools.partial(add_new, i, k - 1) for i in range(4)]
        total = len(work)
        at = [0]

        def hook():
            at[0] += 1
            if extra and at[0] in extra:
                do(*extra[at[0]])
            while work and total - len(work) < -(-total * at[0] // 15):
                work.pop(0)()

        W = join(inverse_factor(A[k, pl.ds(0, BLK), :].reshape(16, 8, BLK), hook))
        while work:
            work.pop(0)()
        WJ[...] = W
        if m > 1:
            top = join(dot3_nt(join(A[k, pl.ds(BLK, BLK), :]), W))
            L[pl.ds(0, BLK), :] = top
            A[k + 1, pl.ds(0, BLK), :] -= dot3_nt(top, top)
        do(*last)

    zp[...] = jnp.zeros(zp.shape, f32)
    zc[...] = jnp.zeros(zc.shape, f32)
    step(0, 8, first=True, extra={1: ("e4",), 5: ("f3",), 10: ("g1",)}, last=("h1",))
    step(1, 7, extra={2: ("f4",), 6: ("g2",)}, last=("h2",))
    step(2, 6, extra={4: ("g3",)}, last=("h3",))
    step(3, 5, extra={4: ("g4",)}, last=("h4",))

    def four(k, carry):
        step(k, 4)
        return carry

    lax.fori_loop(4, 8, four, 0)
    finish(NB - 1, 1)[1]()
    for i in range(4):
        add_new(i, NB - 1)

    columns = rows(me.g * BLK, BLK, BLK)

    def new_copy(p, to):
        return remote(zp.at[rows(to * UNIT, UNIT), :], out.at[:, columns], s_new.at[p], r_new.at[p], me.grp(to))

    each(lambda p: new_copy(p, lax.rem(me.g + p, 16)).start())
    out[:, columns] = zp[rows(me.g * UNIT, UNIT), :]

    new = zc[...]
    pair = dot3(nn, split(new.T * occ[...]), split(new))
    r = lax.broadcasted_iota(jnp.int32, (BLK, BLK), 0)
    c = lax.broadcasted_iota(jnp.int32, (BLK, BLK), 1)
    pair = jnp.where(r // 8 == c // 8, pair, 0.0)
    fold = jnp.where((lax.rem(r, 8) == lax.rem(c, 8)) & (c < UNIT), 1.0, 0.0).astype(bf16)
    hi, lo = split(pair)
    pair = jnp.where(lax.rem(r, 8) == c // 8, nn(hi, fold) + nn(lo, fold), 0.0)
    hi, lo = split(pair)
    atom = jnp.where(r[:8] == c[:8] // 8, 1.0, 0.0).astype(bf16)
    own_rho[...] = nn(atom, hi) + nn(atom, lo)
    mine = rows(me.d * 8, 8)

    def rho_copy(p, to):
        return remote(own_rho, all_rho.at[mine, :], s_rho.at[p], r_rho.at[p], me.dom(to))

    each(lambda p: rho_copy(p, lax.rem(me.d + p, 16)).start())
    all_rho[mine, :] = own_rho[...]
    weight = jnp.broadcast_to(occ[...] * (32768.0 / TOTAL), (8, TOTAL))
    dens[...] = dot3(nn, split(weight), split(zp[...] * zp[...]))[:1]

    def drain(p):
        psi_copy(p, me.g).wait_send()
        dom_copy(p, me.d).wait_send()
        cf_copy(p, me.g).wait_send()
        new_copy(p, me.g).wait()
        rho_copy(p, me.d).wait()

    each(drain)
    for copy in started:
        copy.wait_send()


def on_device(psi, proj, offsets, species, augment_q, rotation, occupation):
    states, cells = psi.shape
    channels = augment_q.shape[1]
    vm, sm, hbm = (pl.BlockSpec(memory_space=s) for s in (pltpu.VMEM, pltpu.SMEM, pl.ANY))
    dma, n = pltpu.SemaphoreType.DMA, len(CHUNK)
    sixteen = [dma((16,)), dma((16,))]
    new_psi, density, rho = pl.pallas_call(
        kernel,
        out_shape=(jax.ShapeDtypeStruct((states, cells), f32), jax.ShapeDtypeStruct((1, BLK), f32),
                   jax.ShapeDtypeStruct((BLK, BLK), f32)),
        in_specs=[hbm, hbm, sm, sm, vm, hbm, vm], out_specs=(vm, vm, vm),
        scratch_shapes=[
            pltpu.VMEM(psi.shape, f32), pltpu.VMEM(proj.shape, f32), pltpu.VMEM(rotation.shape, f32),
            pltpu.VMEM((2, TOTAL, TOTAL), bf16),
            pltpu.VMEM((16, 32, BLK), f32), pltpu.VMEM((16, 32, BLK), f32), pltpu.VMEM((16, 32, BLK), f32),
            pltpu.VMEM((TOTAL, BLK), f32), pltpu.VMEM((TOTAL, BLK), f32),
            pltpu.VMEM((TOTAL, 2 * BLK), bf16), pltpu.VMEM((TOTAL, 2 * BLK), bf16), pltpu.VMEM((NB, 2, UNIT, 2 * BLK), bf16),
            pltpu.VMEM((4, 8, BLK), f32),
            pltpu.VMEM((2, HALF, BLK), f32), pltpu.VMEM((HALF, BLK), f32), pltpu.VMEM((HALF, BLK), f32), pltpu.VMEM((HALF, BLK), f32),
            pltpu.VMEM((8, HALF // 8, BLK), f32), pltpu.VMEM((HALF // 8, BLK), f32),
            pltpu.VMEM((8, HALF // 8, BLK), f32), pltpu.VMEM((HALF // 8, BLK), f32), pltpu.VMEM((HALF // 8, BLK), f32),
            pltpu.VMEM((2, HALF, BLK), f32),
            pltpu.VMEM((PAD, TOTAL, BLK), f32), pltpu.VMEM((PAD * BLK, 2 * BLK), f32),
            pltpu.VMEM((TOTAL, 2 * BLK), bf16), pltpu.VMEM((BLK, 2 * BLK), bf16),
            pltpu.VMEM((BLK, 2 * BLK), bf16), pltpu.VMEM((BLK, 2 * BLK), bf16),
            pltpu.VMEM((TOTAL, BLK), f32), pltpu.VMEM((TOTAL, BLK), f32),
            pltpu.VMEM((8, BLK), f32),
            dma((3,)), *sixteen, *sixteen, *sixteen,
            dma((2 * n,)), dma((2 * n,)), dma((n, 2, 8)), dma((n, 2, 8)), dma((n, 2, 8)), dma((n, 2, 8)), dma((n,)), dma((n,)),
            *sixteen, *sixteen],
        compiler_params=pltpu.CompilerParams(collective_id=0, has_side_effects=True, vmem_limit_bytes=56 * 2**20),
    )(psi, proj, offsets, species, augment_q, rotation, occupation.reshape(1, TOTAL))
    return new_psi, density.reshape(BLK), rho[:, :channels * channels]


def solution(mesh):
    placed = (P("grp", "dom"), P("dom", None, None), P("dom"), P(), P(), P(), P())
    return jax.shard_map(
        on_device, mesh=mesh, in_specs=placed,
        out_specs=(P("grp", "dom"), P(("dom", "grp")), P()), check_vma=False)
```

```python
import functools
import jax
import jax.numpy as jnp
from jax import lax
from jax.experimental import pallas as pl
from jax.experimental.pallas import tpu as pltpu
from jax.sharding import PartitionSpec as P

f32, bf16 = jnp.float32, jnp.bfloat16
MESH = pl.DeviceIdType.MESH
NB = 8
BLK = 128
TOTAL = NB * BLK
UNIT = 64
START = [sum(NB - j for j in range(c)) for c in range(NB + 1)]
CHUNK = (8, 8, 8, 8, 8)
HALF = sum(CHUNK) * UNIT
CH = [u * UNIT for u in CHUNK]
CO = [sum(CH[:c]) for c in range(len(CH) + 1)]
NEAR = 4
PAD = 11


def split(v):
    hi = v.astype(bf16)
    return hi, (v - hi.astype(f32)).astype(bf16)


def nt(a, b):
    return lax.dot_general(a, b, (((1,), (1,)), ((), ())), preferred_element_type=f32)


def nn(a, b):
    return jnp.dot(a, b, preferred_element_type=f32)


def dot3(f, a, b):
    return f(a[0], b[0]) + (f(a[0], b[1]) + f(a[1], b[0]))


def dot3_nt(a, b):
    high = b[:, :BLK]
    return nt(a, jnp.concatenate([high, high], axis=1)) + nt(a[:, :BLK], b[:, BLK:])


def dot3_nn(a, b):
    return nn(a, jnp.concatenate([b[0], b[0]], axis=0)) + nn(a[:, :BLK], b[1])


def join(v):
    return jnp.concatenate(split(v), axis=1)


def rows(first, count, unit=8):
    return pl.ds(pl.multiple_of(first, unit), count)


class Place:
    def __init__(self):
        self.d, self.g = lax.axis_index("dom"), lax.axis_index("grp")
        self.core, self.chip = lax.rem(self.g, 2), self.g // 2
        self.z, self.ylo = self.d // 2, lax.rem(self.d, 2)

    def dom(self, i):
        return {"dom": i, "grp": self.g}

    def grp(self, i):
        return {"dom": self.d, "grp": i}

    def other_core(self):
        return self.grp(self.g + 1 - 2 * self.core)


def greet(me):
    barrier = pltpu.get_barrier_semaphore()

    def one(p, carry):
        pl.semaphore_signal(barrier, inc=1, device_id=me.grp(lax.rem(me.g + p, 16)), device_id_type=MESH)
        pl.semaphore_signal(barrier, inc=1, device_id=me.dom(lax.rem(me.d + p, 16)), device_id_type=MESH)
        return carry

    lax.fori_loop(1, 16, one, 0)
    return lambda: pl.semaphore_wait(barrier, 30)


def remote(src, dst, send, recv, device):
    return pltpu.make_async_remote_copy(
        src_ref=src, dst_ref=dst, send_sem=send, recv_sem=recv, device_id=device, device_id_type=MESH)


def row_b(v, s):
    return jnp.broadcast_to(v[s:s + 1, :], (8, BLK))


def recip(a):
    return pltpu.reciprocal(a, approx=True)


def inverse_factor(V, hook):
    row = lax.broadcasted_iota(jnp.int32, (8, BLK), 0)
    lane = lax.broadcasted_iota(jnp.int32, (8, BLK), 1)
    out = []
    for j in range(16):
        n = min(NEAR, 15 - j)
        col = [jnp.broadcast_to(V[:n + 1, :, 8 * j + t:8 * j + t + 1], (n + 1, 8, BLK)) for t in range(8)]
        D = {(s, t): row_b(col[t][0], s) for t in range(8) for s in range(t, 8)}
        here = lane // 8 == j
        first = jnp.where(here, jnp.where(lane == row + 8 * j, 1.0, 0.0), V[0])
        R = [row_b(first, t) for t in range(8)]
        if n:
            C = [c[1:] for c in col]
            V = jnp.where(here[None], 0.0, V[1:])
            N, F = V[:n], V[n:]
        scale = []
        f = [recip(D[t, t]) for t in range(1, 8, 2)]
        for t0 in range(0, 8, 2):
            t1 = t0 + 1
            a, b, c = D[t0, t0], D[t1, t0], D[t1, t1]
            size = f[t0 // 2]
            det = a * (c * size) - b * (b * size)
            r0 = recip(a)
            r1 = (a * size) * recip(det)
            D[t1, t1] = c - (b * r0) * b
            scale += [lax.rsqrt(a), lax.rsqrt(D[t1, t1])]
            for t, r in ((t0, r0), (t1, r1)):
                l = {s: D[s, t] * r for s in range(t + 1, 8)}
                for s in range(t + 1, 8):
                    for u in range(t + 1, s + 1):
                        if not (s == t1 and t == t0):
                            D[s, u] = D[s, u] - l[s] * D[u, t]
                for s in range(t + 1, 8):
                    R[s] = R[s] - l[s] * R[t]
                if n:
                    li = C[t] * r[None]
                    for u in range(t + 1, 8):
                        C[u] = C[u] - li * D[u, t][None]
                    N = N - li * R[t][None]
        w = R[0] * scale[0]
        for t in range(1, 8):
            w = jnp.where(row == t, R[t] * scale[t], w)
        out.append(jnp.where(lane < 8 * j + 8, w, 0.0))
        if n < 15 - j:
            hi = w.astype(bf16).astype(f32)
            lo = w - hi
            left = jnp.concatenate([hi, hi, lo], axis=0).T[8 * (j + 1 + n):].astype(bf16)
            right = jnp.concatenate([hi, lo, hi], axis=0).astype(bf16)
            F = F - nn(left, right).reshape(15 - j - n, 8, BLK)
            V = jnp.concatenate([N, F], axis=0)
        elif n:
            V = N
        hook()
    return jnp.concatenate(out, axis=0)


def kernel(psi, proj, off, species, aug, rot, occ, out, dens, all_rho,
           psi_v, proj_v, rot_v, rt, placed, got, cp, pc, cf, ps, cs, ws, tiled, t, tp, rc, h, r1, q1, r2, q2, r3, o,
           A, B, L, WJ, YH, YL, zp, zc, own_rho,
           s_in, s_psi, r_psi, s_dom, r_dom, s_cf, r_cf, s_core, r_core, s_x, r_x, s_z, r_z, s_y, r_y, s_new, r_new, s_rho, r_rho):
    me = Place()
    loads = [pltpu.make_async_copy(src, dst, s_in.at[i])
             for i, (src, dst) in enumerate(((psi, psi_v), (proj, proj_v), (rot, rot_v)))]
    for load in loads:
        load.start()
    met = greet(me)
    own = rows(me.g * UNIT, UNIT)

    def psi_copy(p, to):
        return remote(psi.at[:, rows(to * BLK, BLK, BLK)], pc.at[own, :], s_psi.at[p], r_psi.at[p], me.grp(to))

    def dom_copy(p, to):
        return remote(placed.at[to], got.at[p], s_dom.at[p], r_dom.at[p], me.dom(to))

    def cf_copy(p, to):
        return remote(cp.at[me.g], cp.at[me.g], s_cf.at[p], r_cf.at[p], me.grp(to))

    def each(body):
        def one(p, carry):
            body(p)
            return carry
        lax.fori_loop(1, 16, one, 0)

    loads[0].wait()
    loads[1].wait()
    pc[own, :] = psi_v[:, rows(me.g * BLK, BLK, BLK)]
    value = dot3(nt, split(psi_v[...]), split(proj_v[0]))
    value = split(jnp.concatenate([value[:32], value[32:]], axis=1))
    source = lax.broadcasted_iota(jnp.int32, (2 * BLK, BLK), 0)
    lane = lax.broadcasted_iota(jnp.int32, (2 * BLK, BLK), 1)
    gap = jnp.where((source < BLK) == (lane < UNIT), lax.rem(source, BLK) - lax.rem(lane, UNIT), -4096) + off[0] * 8
    for d in range(16):
        pick = jnp.where(gap == UNIT * d, 1.0, 0.0).astype(bf16)
        placed[d] = nn(value[0], pick) + nn(value[1], pick)
    met()
    each(lambda p: dom_copy(p, lax.rem(me.d + p, 16)).start())
    each(lambda p: psi_copy(p, lax.rem(me.g + p, 16)).start())

    A[...] = jnp.zeros(A.shape, f32)
    zp[...] = jnp.zeros(zp.shape, f32)
    zc[...] = jnp.zeros(zc.shape, f32)
    B[pl.ds(TOTAL, (PAD - NB) * BLK), :] = jnp.zeros(((PAD - NB) * BLK, 2 * BLK), f32)
    lane = lax.broadcasted_iota(jnp.int32, (8, BLK), 1)
    repeat = jnp.where(lax.broadcasted_iota(jnp.int32, (8, BLK), 0) == lax.rem(lane, 8), 1.0, 0.0)
    tiled[...] = jnp.dot(aug[...].reshape(32, 8), repeat, precision=lax.Precision.HIGHEST).reshape(4, 8, BLK)
    blocks = [jnp.where(lane // 8 == a, tiled[species[me.d * 8 + a]], 0.0) for a in range(8)]
    blocks.append(jnp.zeros((UNIT, BLK), f32))
    q = split(jnp.concatenate(blocks, axis=0))
    loads[2].wait()

    def turn(i, carry):
        hi, lo = split(rot_v[rows(i * BLK, BLK, BLK), :].T)
        rt[0, :, rows(i * BLK, BLK, BLK)] = hi
        rt[1, :, rows(i * BLK, BLK, BLK)] = lo
        return carry

    lax.fori_loop(0, NB, turn, 0)

    def add_dom(p, total):
        dom_copy(p, me.d).wait_recv()
        return total + got[p]

    started = []
    waits = {}

    def go(copy):
        copy.start()
        started.append(copy)
        return copy

    def arrive(key):
        for copy in waits[key]:
            copy.wait_recv()

    def spread(n, mine, device, source, target, s_sem, r_sem):
        copies = []
        for p in range(1, n):
            to = lax.rem(mine + p, n)
            copies.append(go(remote(source(to), target, s_sem.at[p], r_sem.at[p], device(to))))
        return copies

    def chips(c, i, source, target):
        return spread(8, me.chip, lambda to: me.grp(to * 2 + me.core), source, target, s_x.at[c, i], r_x.at[c, i])

    def along_z(c, i, source, target):
        return spread(8, me.z, lambda to: me.dom(to * 2 + me.ylo), source, target, s_z.at[c, i], r_z.at[c, i])

    def sizes(c):
        return CO[c], CH[c], CO[c] // 8, CH[c] // 8

    def step_a(c):
        chunk = pl.ds(CO[c], CH[c])
        waits["a", c] = [go(remote(t.at[1 - me.core, chunk], rc.at[chunk], s_core.at[c], r_core.at[c], me.other_core()))]

    def step_b(c):
        arrive(("a", c))
        first, count, at, n = sizes(c)
        chunk = pl.ds(first, count)
        h[chunk] = t[me.core, chunk] + rc[chunk]
        waits["b", c] = chips(c, 0, lambda to: h.at[rows(first + to * n, n)], r1.at[me.chip, pl.ds(at, n)])

    def step_c(c):
        arrive(("b", c))
        first, count, at, n = sizes(c)
        mine, part = rows(first + me.chip * n, n), pl.ds(at, n)
        r1[me.chip, part] = h[mine] + tp[mine]
        total = r1[0, part]
        for i in range(1, 8):
            total = total + r1[i, part]
        q1[part] = total
        m = n // 8
        waits["c", c] = along_z(c, 0, lambda to: q1.at[rows(at + to * m, m)], r2.at[me.z, pl.ds(at, m)])

    def step_d(c):
        arrive(("c", c))
        first, count, at, n = sizes(c)
        m = n // 8
        part = pl.ds(at, m)
        r2[me.z, part] = q1[rows(at + me.z * m, m)]
        total = r2[0, part]
        for i in range(1, 8):
            total = total + r2[i, part]
        q2[part] = total
        waits["d", c] = [go(remote(q2.at[part], r3.at[part], s_y.at[c], r_y.at[c], me.dom(me.d + 1 - 2 * me.ylo)))]

    def step_e(c):
        arrive(("d", c))
        first, count, at, n = sizes(c)
        m = n // 8
        here = o.at[me.core, rows(first + me.chip * n + me.z * m, m)]
        here[...] = q2[pl.ds(at, m)] + r3[pl.ds(at, m)]
        waits["e", c] = along_z(c, 1, lambda to: here, here)

    def step_f(c):
        arrive(("e", c))
        first, count, at, n = sizes(c)
        here = o.at[me.core, rows(first + me.chip * n, n)]
        waits["f", c] = chips(c, 1, lambda to: here, here)

    def step_g(c):
        arrive(("f", c))
        here = o.at[me.core, pl.ds(CO[c], CH[c])]
        n = len(CHUNK) + c
        waits["g", c] = [go(remote(here, here, s_core.at[n], r_core.at[n], me.other_core()))]

    def step_h(c):
        arrive(("g", c))
        for col in range(NB):
            for r in range(NB - col):
                unit = START[col] + r
                if CO[c] <= unit * UNIT < CO[c + 1]:
                    for half in range(2):
                        A[col, BLK * r + UNIT * half:BLK * r + UNIT * half + UNIT] += o[half, pl.ds(unit * UNIT, UNIT)]

    def do(*names):
        for name in names:
            {"a": step_a, "b": step_b, "c": step_c, "d": step_d, "e": step_e, "f": step_f, "g": step_g, "h": step_h}[name[0]](int(name[1]))

    def gram_of_psi():
        ready = 0
        padding = pl.ds(START[NB] * UNIT, HALF - START[NB] * UNIT)
        t[:, padding] = jnp.zeros((2, HALF - START[NB] * UNIT, BLK), f32)
        tp[padding] = jnp.zeros((HALF - START[NB] * UNIT, BLK), f32)
        for c in range(NB):
            part = dot3_nt(ps[BLK * c:], ps[BLK * c:BLK * c + BLK])
            for r in range(NB - c):
                for half in range(2):
                    t[half, pl.ds(UNIT * (START[c] + r), UNIT)] = part[BLK * r + UNIT * half: BLK * r + UNIT * half + UNIT]
            while ready < len(CHUNK) and (CO[ready + 1] <= START[c + 1] * UNIT or c == NB - 1):
                step_a(ready)
                ready += 1

    cp[me.g] = lax.fori_loop(1, 16, add_dom, placed[me.d])
    each(lambda p: cf_copy(p, lax.rem(me.g + p, 16)).start())

    each(lambda p: psi_copy(p, me.g).wait_recv())
    ps[...] = join(pc[...])
    gram_of_psi()
    do("b0", "b1", "b2", "b3", "b4")
    B[:TOTAL, :BLK] = pc[...]

    each(lambda p: cf_copy(p, me.g).wait_recv())
    left = lax.broadcasted_iota(jnp.int32, (32, BLK), 1) < UNIT
    for g in range(16):
        cf[UNIT * g:UNIT * g + 32] = jnp.where(left, cp[g], 0.0)
        cf[UNIT * g + 32:UNIT * g + 64] = jnp.where(left, pltpu.roll(cp[g], UNIT, 1), 0.0)
    cs[...] = join(cf[...])
    ws[...] = join(dot3(nn, split(cf[...]), q)).reshape(NB, 2, UNIT, 2 * BLK)
    for c in range(NB):
        own_rows = ws[c:, me.core].reshape((NB - c) * UNIT, 2 * BLK)
        tp[pl.ds(START[c] * UNIT, (NB - c) * UNIT)] = dot3_nt(own_rows, cs[BLK * c:BLK * c + BLK])
        if c == 0:
            do("c0")
    do("c1")
    B[:TOTAL, BLK:] = cf[...]
    do("c2", "d0", "c3", "d1", "e0", "e1", "d2", "c4", "e2", "f0", "d3", "f1", "e3", "d4", "f2", "g0", "h0")

    def add_new(i, k):
        piece, past = pl.ds(2 * BLK * i, 2 * BLK), rows(k * BLK, BLK, BLK)
        new = dot3_nn(jnp.concatenate([rt[0, piece, past], rt[1, piece, past]], axis=1), (YH[...], YL[...]))
        zp[piece] += new[:, :BLK]
        zc[piece] += new[:, BLK:]

    def finish(k, m):
        def panel(a, n):
            past = A[k, pl.ds(BLK * (a + 1), BLK * n), :]
            L[pl.ds(BLK * a, BLK * n), :] = join(dot3_nt(join(past), WJ[...]))

        def substitute():
            hi, lo = split(dot3_nn(WJ[...], split(B[rows(k * BLK, BLK), :])))
            YH[...] = hi
            YL[...] = lo

        return [functools.partial(panel, a, min(2, m - a)) for a in range(1, m, 2)], substitute

    def step(k, m, first=False, extra=None, last=()):
        work = []

        def column(b):
            n = m - b if b else m - 1
            a = b if b else 1
            A[k + b, pl.ds(BLK * (a - b), BLK * n), :] -= dot3_nt(L[pl.ds(BLK * a, BLK * n), :], L[pl.ds(BLK * b, BLK), :])

        def right(a):
            B[rows((k + a) * BLK, BLK), :] -= dot3_nn(L[pl.ds(BLK * a, BLK), :], (YH[...], YL[...]))

        if not first:
            panels, substitute = finish(k - 1, m)
            work += panels
            work.append(functools.partial(column, 0))
            work.append(substitute)
            work.append(functools.partial(right, 0))
            work += [functools.partial(column, b) for b in range(1, m)]
            work += [functools.partial(right, a) for a in range(1, m)]
            work += [functools.partial(add_new, i, k - 1) for i in range(4)]
        total = len(work)
        at = [0]

        def hook():
            at[0] += 1
            if extra and at[0] in extra:
                do(*extra[at[0]])
            while work and total - len(work) < -(-total * at[0] // 15):
                work.pop(0)()

        W = join(inverse_factor(A[k, pl.ds(0, BLK), :].reshape(16, 8, BLK), hook))
        while work:
            work.pop(0)()
        WJ[...] = W
        if m > 1:
            top = join(dot3_nt(join(A[k, pl.ds(BLK, BLK), :]), W))
            L[pl.ds(0, BLK), :] = top
            A[k + 1, pl.ds(0, BLK), :] -= dot3_nt(top, top)
        do(*last)

    step(0, 8, first=True, extra={1: ("e4",), 5: ("f3",), 10: ("g1",)}, last=("h1",))
    step(1, 7, extra={2: ("f4",), 6: ("g2",)}, last=("h2",))
    step(2, 6, extra={4: ("g3",)}, last=("h3",))
    step(3, 5, extra={4: ("g4",)}, last=("h4",))

    def four(k, carry):
        step(k, 4)
        return carry

    lax.fori_loop(4, 8, four, 0)
    finish(NB - 1, 1)[1]()
    columns = rows(me.g * BLK, BLK, BLK)

    def new_copy(p, to):
        return remote(zp.at[rows(to * UNIT, UNIT), :], out.at[:, columns], s_new.at[p], r_new.at[p], me.grp(to))

    for i in range(4):
        add_new(i, NB - 1)
        for to in range(4 * i, 4 * i + 4):
            @pl.when(me.g != to)
            def _():
                new_copy(lax.rem(to - me.g + 16, 16), to).start()

    out[:, columns] = zp[rows(me.g * UNIT, UNIT), :]

    new = zc[...]
    pair = dot3(nn, split(new.T * occ[...]), split(new))
    r = lax.broadcasted_iota(jnp.int32, (BLK, BLK), 0)
    c = lax.broadcasted_iota(jnp.int32, (BLK, BLK), 1)
    pair = jnp.where(r // 8 == c // 8, pair, 0.0)
    fold = jnp.where((lax.rem(r, 8) == lax.rem(c, 8)) & (c < UNIT), 1.0, 0.0).astype(bf16)
    hi, lo = split(pair)
    pair = jnp.where(lax.rem(r, 8) == c // 8, nn(hi, fold) + nn(lo, fold), 0.0)
    hi, lo = split(pair)
    atom = jnp.where(r[:8] == c[:8] // 8, 1.0, 0.0).astype(bf16)
    own_rho[...] = nn(atom, hi) + nn(atom, lo)
    mine = rows(me.d * 8, 8)

    def rho_copy(p, to):
        return remote(own_rho, all_rho.at[mine, :], s_rho.at[p], r_rho.at[p], me.dom(to))

    each(lambda p: rho_copy(p, lax.rem(me.d + p, 16)).start())
    all_rho[mine, :] = own_rho[...]
    weight = jnp.broadcast_to(occ[...] * (32768.0 / TOTAL), (8, TOTAL))
    dens[...] = dot3(nn, split(weight), split(zp[...] * zp[...]))[:1]

    def drain(p):
        psi_copy(p, me.g).wait_send()
        dom_copy(p, me.d).wait_send()
        cf_copy(p, me.g).wait_send()
        new_copy(p, me.g).wait()
        rho_copy(p, me.d).wait()

    each(drain)
    for copy in started:
        copy.wait_send()


def on_device(psi, proj, offsets, species, augment_q, rotation, occupation):
    states, cells = psi.shape
    channels = augment_q.shape[1]
    vm, sm, hbm = (pl.BlockSpec(memory_space=s) for s in (pltpu.VMEM, pltpu.SMEM, pl.ANY))
    dma, n = pltpu.SemaphoreType.DMA, len(CHUNK)
    sixteen = [dma((16,)), dma((16,))]
    new_psi, density, rho = pl.pallas_call(
        kernel,
        out_shape=(jax.ShapeDtypeStruct((states, cells), f32), jax.ShapeDtypeStruct((1, BLK), f32),
                   jax.ShapeDtypeStruct((BLK, BLK), f32)),
        in_specs=[hbm, hbm, sm, sm, vm, hbm, vm], out_specs=(vm, vm, vm),
        scratch_shapes=[
            pltpu.VMEM(psi.shape, f32), pltpu.VMEM(proj.shape, f32), pltpu.VMEM(rotation.shape, f32),
            pltpu.VMEM((2, TOTAL, TOTAL), bf16),
            pltpu.VMEM((16, 32, BLK), f32), pltpu.VMEM((16, 32, BLK), f32), pltpu.VMEM((16, 32, BLK), f32),
            pltpu.VMEM((TOTAL, BLK), f32), pltpu.VMEM((TOTAL, BLK), f32),
            pltpu.VMEM((TOTAL, 2 * BLK), bf16), pltpu.VMEM((TOTAL, 2 * BLK), bf16), pltpu.VMEM((NB, 2, UNIT, 2 * BLK), bf16),
            pltpu.VMEM((4, 8, BLK), f32),
            pltpu.VMEM((2, HALF, BLK), f32), pltpu.VMEM((HALF, BLK), f32), pltpu.VMEM((HALF, BLK), f32), pltpu.VMEM((HALF, BLK), f32),
            pltpu.VMEM((8, HALF // 8, BLK), f32), pltpu.VMEM((HALF // 8, BLK), f32),
            pltpu.VMEM((8, HALF // 8, BLK), f32), pltpu.VMEM((HALF // 8, BLK), f32), pltpu.VMEM((HALF // 8, BLK), f32),
            pltpu.VMEM((2, HALF, BLK), f32),
            pltpu.VMEM((PAD, TOTAL, BLK), f32), pltpu.VMEM((PAD * BLK, 2 * BLK), f32),
            pltpu.VMEM((TOTAL, 2 * BLK), bf16), pltpu.VMEM((BLK, 2 * BLK), bf16),
            pltpu.VMEM((BLK, 2 * BLK), bf16), pltpu.VMEM((BLK, 2 * BLK), bf16),
            pltpu.VMEM((TOTAL, BLK), f32), pltpu.VMEM((TOTAL, BLK), f32),
            pltpu.VMEM((8, BLK), f32),
            dma((3,)), *sixteen, *sixteen, *sixteen,
            dma((2 * n,)), dma((2 * n,)), dma((n, 2, 8)), dma((n, 2, 8)), dma((n, 2, 8)), dma((n, 2, 8)), dma((n,)), dma((n,)),
            *sixteen, *sixteen],
        compiler_params=pltpu.CompilerParams(collective_id=0, has_side_effects=True, vmem_limit_bytes=56 * 2**20),
    )(psi, proj, offsets, species, augment_q, rotation, occupation.reshape(1, TOTAL))
    return new_psi, density.reshape(BLK), rho[:, :channels * channels]


def solution(mesh):
    placed = (P("grp", "dom"), P("dom", None, None), P("dom"), P(), P(), P(), P())
    return jax.shard_map(
        on_device, mesh=mesh, in_specs=placed,
        out_specs=(P("grp", "dom"), P(("dom", "grp")), P()), check_vma=False)
```
